128 devices in a mesh: dp: 32 (over x, y, core), tp: 4 (over z).
Axes of the slice: x: 4, y: 4, z: 4, core: 2. Of those that a mesh axis runs over, the one named last changes fastest.
Arguments:
- query: bfloat16 [128, 64, 576], P('dp', 'tp'), may hold values from -65 to 65
- new_latent: bfloat16 [128, 576], P('dp'), may hold values from -4 to 4
- cache: bfloat16 [64, 1024, 576], P('dp'), may hold values from -4 to 4
- cache_len: int32 [64], P('dp'), may hold values from 128 to 1024, as said below
- w_uv: bfloat16 [64, 512, 128], P('tp'), may hold values from -1.5 to 1.5
- w_out: bfloat16 [8192, 7168], P('tp', 'dp'), may hold values from -0.0625 to 0.0625
- hidden_in: bfloat16 [128, 7168], P('tp', 'dp'), may hold values from -25 to 25
- norm_gain: float32 [7168], P('dp'), may hold values from 0.1 to 1.9
- routing: int32 [128, 8], replicated, may hold values from 0 to 15, all different within a row; in each aligned block of 32 rows (0 to 31, 32 to 63, ...) at most 24 rows name the same one
- route_weight: float32 [128, 8], replicated, may hold values from 0.1 to 0.6
- w_gate_up: bfloat16 [2, 7168, 32768], P(None, None, ('dp', 'tp')), may hold values from -0.0625 to 0.0625
- w_down: bfloat16 [32768, 7168], P(('dp', 'tp')), may hold values from -0.125 to 0.125
Outputs:
- hidden_out: bfloat16 [128, 7168], P('tp', 'dp')
The draws below stay inside these ranges and needn't reach their ends.
Inputs may be any that keep to these rules, and one draw needn't show every extreme that they name: `routing`: each row names 8 different experts. Within each aligned block of 32 rows no expert is named by more than 24 rows, a bound that some block reaches. `cache_len`: some request holds a full cache of 1024 tokens.
All inputs are finite; a program needn't handle non-finite values.
Results may differ from the reference program's by a relative error of at most 0.006.
Values may be sent and summed in bfloat16 or wider, within the bound.
A program may use at most 128 MiB of HBM per device.

```python
import math
import jax
import jax.numpy as jnp
import numpy as np
from jax import lax

D = 7168
FF = 2048
KVL = 512
ROPE = 64
VH = 128
HEADS = 64
EXPERTS = 16
TOP = 8
MAXLEN = 1024
LAT = 576
REQS = 64
TOKENS = 128
QTOK = 32
CAP = 24


def draw_cache(key, part):
    own_key = jax.random.fold_in(key, 11)
    return jnp.clip(jax.random.normal(own_key, (REQS, MAXLEN, KVL + ROPE), jnp.float32), -4.0, 4.0).astype(jnp.bfloat16)


def draw_query(key, part):
    own_key = jax.random.fold_in(key, 13)
    return jnp.clip(jax.random.normal(own_key, (TOKENS, HEADS, KVL + ROPE), jnp.float32), -4.0, 4.0).astype(jnp.bfloat16)


def draw_cache_len(key, part):
    own_key = jax.random.fold_in(key, 17)
    lengths = jax.random.randint(own_key, (REQS,), MAXLEN // 8, MAXLEN + 1)
    longest = jax.random.randint(jax.random.fold_in(own_key, 1), (), 0, REQS)
    return lengths.at[longest].set(MAXLEN)


def draw_hidden_in(key, part):
    own_key = jax.random.fold_in(key, 19)
    rising = 0.6 * jnp.exp(math.log(3.0) * jnp.arange(D, dtype=jnp.float32) / D)
    return (jnp.clip(jax.random.normal(own_key, (TOKENS, D), jnp.float32), -4.0, 4.0) * rising[None, :]).astype(jnp.bfloat16)


def level_of(stream_key, extent, shards, smallest, high):
    gain, own = 1.0, jax.random.fold_in(stream_key, 6)
    for dim, blocks in shards:
        steps = jnp.exp(jax.random.uniform(jax.random.fold_in(own, dim), (blocks,), jnp.float32, smallest / len(shards), high / len(shards)))
        gain = gain * jnp.repeat(steps, extent[dim] // blocks).reshape([-1 if axis == dim else 1 for axis in range(len(extent))])
    return gain


def shared_out(rng, own, number, rows, amount, top, reach, lean):
    sequence = jax.random.permutation(rng, amount)
    packed, usual = portions_of(amount, rows * top, reach, lean, True), portions_of(amount, rows * top, reach, lean, False)
    places = jnp.arange(amount)

    def named(tallies, offset_by):
        used = int((tallies > 0).sum())
        fixed = max(1, used // 4)
        shifted = fixed + (places - fixed + offset_by * (used - fixed)) % max(1, amount - fixed)
        return jnp.zeros((amount,), jnp.int32).at[sequence[jnp.where(places < fixed, places, shifted)]].set(jnp.asarray(tallies, jnp.int32))

    tallies = jnp.where(number % 4 == 0, named(packed, number // 4), named(usual, number - number // 4 - 1))
    mixed = jax.random.permutation(jax.random.fold_in(own, 3), amount)
    giver, receiver = mixed[0:amount // 2 * 2:2], mixed[1:amount // 2 * 2:2]
    room = jnp.minimum(tallies[giver] - 1, reach - tallies[receiver]) // 2
    room = jnp.where((giver == sequence[0]) | (receiver == sequence[0]) | (tallies[receiver] == 0), 0, jnp.maximum(room, 0))
    shifted = jax.random.randint(jax.random.fold_in(own, 4), (amount // 2,), 0, 1 << 20) % (room + 1)
    tallies = tallies.at[giver].add(-shifted).at[receiver].add(shifted)
    members = jnp.searchsorted(jnp.cumsum(tallies), jnp.arange(rows * top), side="right").astype(jnp.int32)
    table = members.reshape(top, rows).T
    table = table[jax.random.permutation(jax.random.fold_in(own, 1), rows)]
    offset_by = jax.random.randint(jax.random.fold_in(own, 2), (rows, 1), 0, top)
    return jnp.take_along_axis(table, (jnp.arange(top)[None, :] + offset_by) % top, axis=1)


def portions_of(number_of, total, most, slope, full):
    portions = [(1 << 20) // math.isqrt(grade ** slope) + 1 for grade in range(1, number_of + 1)]
    largest = most if full else min(most, max(-(-total // number_of), total * portions[0] // sum(portions)))
    least = 1 if total - largest >= number_of - 1 else 0
    given, spare = [largest] + [least] * (number_of - 1), total - largest - least * (number_of - 1)
    while spare > 0:
        movable = [i for i in range(1, number_of) if given[i] < largest] or [i for i in range(1, number_of) if given[i] < most]
        mass, left = sum([portions[i] for i in movable]), spare
        for i in movable:
            extra = min(most - given[i], max(1, left * portions[i] // mass), spare)
            given[i] = given[i] + extra
            spare = spare - extra
    return np.array(given)


def noise(key, extent, spread, bound, pieces=(), kind=jnp.bfloat16):
    values = jax.random.normal(key, extent, jnp.float32) * spread
    if len(pieces) > 0:
        values = level_of(key, extent, pieces, -0.22, 0.18) * values
    return jnp.clip(values, min=-bound, max=bound).astype(kind)


def setup_inputs(seed: int = 0) -> dict:
    streams_of = jax.random.split(jax.random.key(seed), 13)
    query = draw_query(jax.random.fold_in(streams_of[12], 71), 0)
    new_latent = noise(streams_of[1], (TOKENS, LAT), 1.0, 4.0, ((0, 32),))
    cache = draw_cache(jax.random.fold_in(streams_of[12], 71), 0)
    cache_len = draw_cache_len(jax.random.fold_in(streams_of[12], 71), 0)
    w_uv = noise(streams_of[4], (HEADS, KVL, VH), (KVL // 32) ** -0.5, 1.5, ((0, 4),))
    w_out = noise(streams_of[5], (HEADS * VH, D), (HEADS * VH) ** -0.5, 0.0625, ((0, 4), (1, 32)))
    hidden_in = draw_hidden_in(jax.random.fold_in(streams_of[12], 71), 0)
    norm_gain = jnp.clip(1.0 + 0.18 * jax.random.normal(streams_of[7], (D,), jnp.float32), 0.1, 1.9)
    routing_keys = jax.random.split(jax.random.fold_in(streams_of[8], 1), TOKENS // QTOK)
    routing_turns = jax.random.permutation(jax.random.fold_in(streams_of[8], 3), TOKENS // QTOK)
    routing = jax.vmap(lambda own, number: shared_out(jax.random.fold_in(streams_of[8], 2), own, number, QTOK, EXPERTS, TOP, CAP, 1))(routing_keys, routing_turns).reshape((TOKENS, TOP))
    route_weight = jnp.clip(jnp.exp(jax.random.uniform(streams_of[9], (TOKENS, TOP), jnp.float32, math.log(0.1), math.log(0.6))), 0.1, 0.6)
    w_gate_up = noise(streams_of[10], (2, D, EXPERTS * FF), D ** -0.5, 0.0625, ((2, 128),))
    w_down = noise(streams_of[11], (EXPERTS * FF, D), FF ** -0.5, 0.125, ((0, 128),))
    return dict(query=query, new_latent=new_latent, cache=cache, cache_len=cache_len, w_uv=w_uv, w_out=w_out, hidden_in=hidden_in, norm_gain=norm_gain, routing=routing, route_weight=route_weight, w_gate_up=w_gate_up, w_down=w_down)


def attend(query, new_latent, cache, cache_len):
    scale = float(VH + ROPE) ** (-0.5)
    grid = query.astype(jnp.float32).reshape(REQS, 2, HEADS, KVL + ROPE)
    keys = cache.astype(jnp.float32)
    fresh = new_latent.astype(jnp.float32).reshape(REQS, 2, KVL + ROPE)
    far = jnp.einsum('bthc,blc->bthl', grid, keys) * scale
    live = jnp.arange(MAXLEN, dtype=jnp.int32)[None, :] < cache_len[:, None]
    far = jnp.where(live[:, None, None, :], far, -jnp.inf)
    near = jnp.einsum('bthc,buc->bthu', grid, fresh) * scale
    causal = jnp.arange(2, dtype=jnp.int32)[:, None] >= jnp.arange(2, dtype=jnp.int32)[None, :]
    near = jnp.where(causal[None, :, None, :], near, -jnp.inf)
    scores = jnp.concatenate([far, near], axis=-1)
    highest = lax.optimization_barrier(jnp.max(scores, axis=-1, keepdims=True))
    weights = jnp.exp(scores - highest)
    probs = (weights / lax.optimization_barrier(jnp.sum(weights, axis=-1, keepdims=True))).astype(jnp.bfloat16)
    probs = lax.optimization_barrier(probs).astype(jnp.float32)
    values = jnp.concatenate([keys[:, :, :KVL], fresh[:, :, :KVL]], axis=1)
    context = jnp.einsum('bthl,blc->bthc', probs, values)
    return context.astype(jnp.bfloat16).reshape(TOKENS, HEADS, KVL)

def reference(query, new_latent, cache, cache_len, w_uv, w_out, hidden_in, norm_gain, routing, route_weight, w_gate_up, w_down):
    context = attend(query, new_latent, cache, cache_len)
    head_out = jnp.einsum('ihc,hcv->ihv', context.astype(jnp.float32), w_uv.astype(jnp.float32))
    head_out = head_out.astype(jnp.bfloat16).reshape(TOKENS, HEADS * VH)
    mid = hidden_in.astype(jnp.float32) + jnp.dot(head_out, w_out, preferred_element_type=jnp.float32)
    power = lax.optimization_barrier(jnp.mean(mid * mid, axis=1, keepdims=True))
    normed = (mid * lax.rsqrt(power + 1e-06) * norm_gain.astype(jnp.float32)[None, :]).astype(jnp.bfloat16)
    chosen = routing[:, :, None] == jnp.arange(EXPERTS, dtype=jnp.int32)[None, None, :]
    mixing = lax.optimization_barrier(jnp.sum(jnp.where(chosen, route_weight[:, :, None], 0.0), axis=1))

    def one_expert(running, index):
        first_unit = (index * FF).astype(jnp.int32)
        gate_cols = lax.dynamic_slice_in_dim(w_gate_up[0], first_unit, FF, 1)
        up_cols = lax.dynamic_slice_in_dim(w_gate_up[1], first_unit, FF, 1)
        down_rows = lax.dynamic_slice_in_dim(w_down, first_unit, FF, 0)
        gate_part = jnp.dot(normed, gate_cols, preferred_element_type=jnp.float32)
        up_part = jnp.dot(normed, up_cols, preferred_element_type=jnp.float32)
        hidden_act = (jax.nn.silu(gate_part) * up_part).astype(jnp.bfloat16)
        result = jnp.dot(hidden_act, down_rows, preferred_element_type=jnp.float32)
        share = lax.dynamic_slice_in_dim(mixing, index.astype(jnp.int32), 1, 1)
        return (running + share * result, None)
    moe_out, _ = lax.scan(one_expert, jnp.zeros((TOKENS, D), jnp.float32), jnp.arange(EXPERTS, dtype=jnp.int32))
    return (mid + moe_out).astype(jnp.bfloat16)
```

```python
import jax
import jax.numpy as jnp
from jax import lax
from jax.experimental import pallas as pl
from jax.experimental.pallas import tpu as pltpu
from jax.sharding import PartitionSpec as P

D = 7168
LAT = 576
KVL = 512
ROPE = 64
VH = 128
MAXLEN = 1024
EXPERTS = 16
TOKENS = 128
TOP = 8
QTOK = 32
CAP = 24
ROWS = 4 * CAP
COLS = 224
WIDE = 256
UNITS = 256
XY = 16
EPSILON = 1e-06
MESH = pl.DeviceIdType.MESH
F32 = jnp.float32
BF16 = jnp.bfloat16


def mm(a, b, dims=((1,), (0,)), precision=None):
    return lax.dot_general(a, b, (dims, ((), ())), preferred_element_type=F32, precision=precision)


def kernel(
    query, new_latent, cache, cache_len, w_uv, w_out, hidden_in, gain, routing, route_weight,
    w_gate_up, w_down, out,
    cache_v, uv_v, out_v, gu_v, down_v,
    heads, heads32, part, part_in, rows_z, pick, pick_t, mem_t, pos_t, mid_s, wcol,
    x_out, x_in, gate_s, up_s, sq_s, act_s, y_mine, y_sib, y_out, y_in, fin, fin_in,
    load_sem, a_s, a_r, a2_s, a2_r, c_s, c_r, d_s, d_r, e_s, e_r, e2_s, e2_r,
    g_s, g_r, g2_s, g2_r, h_s, h_r,
):
    dp = lax.axis_index("dp")
    z = lax.axis_index("tp")
    xy = dp // 2
    core = dp % 2
    sib = xy * 2 + (1 - core)

    def peer(k):
        return (xy + k) % XY

    def source(k):
        return (xy + XY - k) % XY

    def zpeer(j):
        return (z + j) % 4

    def remote(src, dst, send, recv, to_dp, to_z):
        return pltpu.make_async_remote_copy(
            src_ref=src, dst_ref=dst, send_sem=send, recv_sem=recv,
            device_id=(to_dp, to_z), device_id_type=MESH,
        )

    barrier = pltpu.get_barrier_semaphore()

    def greet(k, _):
        pl.semaphore_signal(barrier, inc=1, device_id=(peer(k) * 2 + core, z), device_id_type=MESH)
        return 0

    pl.semaphore_signal(barrier, inc=1, device_id=(sib, z), device_id_type=MESH)
    lax.fori_loop(1, XY, greet, 0)
    for j in range(1, 4):
        pl.semaphore_signal(barrier, inc=1, device_id=(dp, zpeer(j)), device_id_type=MESH)

    loads = [
        pltpu.make_async_copy(cache.at[0], cache_v.at[0], load_sem.at[0]),
        pltpu.make_async_copy(cache.at[1], cache_v.at[1], load_sem.at[1]),
        pltpu.make_async_copy(w_uv, uv_v, load_sem.at[2]),
        pltpu.make_async_copy(w_out, out_v, load_sem.at[3]),
        pltpu.make_async_copy(w_gate_up, gu_v, load_sem.at[4]),
        pltpu.make_async_copy(w_down, down_v, load_sem.at[5]),
    ]
    for copy in loads:
        copy.start()

    scale = float(VH + ROPE) ** (-0.5)
    q_all = query[...].reshape(4 * XY, LAT)
    fresh = new_latent[...]
    near = mm(q_all, fresh, ((1,), (1,))) * scale
    row = lax.broadcasted_iota(jnp.int32, (64, 4), 0)
    col = lax.broadcasted_iota(jnp.int32, (64, 4), 1)
    near = jnp.where((row // 32 == col // 2) & (row // 16 >= col), near, -jnp.inf)
    contexts = []
    for b in range(2):
        loads[b].wait()
        q = q_all[32 * b : 32 * b + 32]
        far = mm(q, cache_v[b], ((1,), (1,))) * scale
        place = lax.broadcasted_iota(jnp.int32, (32, MAXLEN), 1)
        far = jnp.where(place < cache_len[b], far, -jnp.inf)
        close = near[32 * b : 32 * b + 32]
        highest = jnp.maximum(
            jnp.max(far, axis=1, keepdims=True), jnp.max(close, axis=1, keepdims=True)
        )
        far = jnp.exp(far - highest)
        close = jnp.exp(close - highest)
        total = jnp.sum(far, axis=1, keepdims=True) + jnp.sum(close, axis=1, keepdims=True)
        context = mm((far / total).astype(BF16), cache_v[b, :, :KVL])
        context = context + mm((close / total).astype(BF16), fresh[:, :KVL])
        contexts.append(context.astype(BF16))
    context = jnp.concatenate(contexts, axis=0)
    loads[2].wait()
    row = lax.broadcasted_iota(jnp.int32, (64, VH), 0)
    head_out = jnp.zeros((64, VH), F32)
    for h in range(16):
        head_out = jnp.where(row % 16 == h, mm(context, uv_v[h]), head_out)
    heads[dp] = head_out.astype(BF16)

    pl.semaphore_wait(barrier, XY + 3)

    def a_copy(k):
        return remote(heads.at[dp], heads.at[dp], a_s.at[k], a_r.at[k], peer(k) * 2 + core, z)

    def a2_copy(k):
        which = source(k) * 2 + core
        return remote(heads.at[which], heads.at[which], a2_s.at[k], a2_r.at[k], sib, z)

    def a_start(k, _):
        a_copy(k).start()
        return 0

    lax.fori_loop(1, XY, a_start, 0)
    a2_copy(0).start()

    lane16 = lax.broadcasted_iota(jnp.int32, (TOKENS, EXPERTS), 1)
    member = jnp.zeros((TOKENS, EXPERTS), F32)
    share = jnp.zeros((TOKENS, 1), F32)
    for k in range(TOP):
        named = routing[:, k : k + 1]
        member = member + jnp.where(named == lane16, 1.0, 0.0)
        share = share + jnp.where(named == xy, route_weight[:, k : k + 1], 0.0)
    member = member.astype(BF16)
    i0 = lax.broadcasted_iota(jnp.int32, (TOKENS, TOKENS), 0)
    i1 = lax.broadcasted_iota(jnp.int32, (TOKENS, TOKENS), 1)
    eye = jnp.where(i0 == i1, 1.0, 0.0).astype(BF16)
    earlier = jnp.where((i0 < i1) & (i0 // QTOK == i1 // QTOK), 1.0, 0.0).astype(BF16)
    mem_t[...] = mm(member, eye, ((0,), (0,)))
    pos_t[...] = mm(member, earlier, ((0,), (0,)))
    slot = lax.broadcasted_iota(jnp.int32, (ROWS, TOKENS), 0)
    token = lax.broadcasted_iota(jnp.int32, (ROWS, TOKENS), 1)
    in_block = slot // CAP == token // QTOK
    rank = (slot % CAP).astype(F32)

    def tables(e, _):
        here = (mem_t[pl.ds(e, 1), :] > 0.5) & in_block & (pos_t[pl.ds(e, 1), :] == rank)
        chosen = jnp.where(here, 1.0, 0.0).astype(BF16)
        pick[e] = chosen
        pick_t[e] = mm(eye, chosen, ((1,), (1,))).astype(BF16)
        return 0

    lax.fori_loop(0, EXPERTS, tables, 0)
    wcol[...] = mm(
        pick[xy].astype(F32), jnp.broadcast_to(share, (TOKENS, 128)), precision=lax.Precision.HIGHEST
    )

    def a_forward(k, _):
        a_copy(k).wait_recv()
        a2_copy(k).start()
        return 0

    lax.fori_loop(1, XY, a_forward, 0)

    def a_finish(k, _):
        a2_copy(k).wait_recv()
        return 0

    lax.fori_loop(0, XY, a_finish, 0)

    heads32[...] = heads[...].reshape(32 * 64, VH).astype(F32)
    loads[3].wait()
    projected = jnp.zeros((TOKENS, COLS), F32)
    for h in range(16):
        lhs = heads32[pl.ds(h, TOKENS, stride=16), :].astype(BF16)
        projected = projected + mm(lhs, out_v[VH * h : VH * (h + 1), :])
    for q in range(4):
        part[q, :, :COLS] = projected[QTOK * q : QTOK * (q + 1)]
        part[q, :, COLS:] = jnp.zeros((QTOK, WIDE - COLS), F32)

    def c_copy(j):
        return remote(part.at[zpeer(j)], part_in.at[z], c_s.at[j], c_r.at[j], dp, zpeer(j))

    for j in range(1, 4):
        c_copy(j).start()
    mid = part[z][:, :COLS] + hidden_in[...].astype(F32)
    for j in range(1, 4):
        c_copy(j).wait_recv()
        mid = mid + part_in[zpeer(4 - j)][:, :COLS]
    mid_s[...] = mid
    square = jnp.sum(mid * mid, axis=1, keepdims=True)
    square_hi = square.astype(BF16)
    square_lo = (square - square_hi.astype(F32)).astype(BF16)
    rows_z[z, :, :COLS] = (mid * gain[...]).astype(BF16)
    lane = lax.broadcasted_iota(jnp.int32, (QTOK, WIDE - COLS), 1)
    spare = jnp.where(lane == 0, square_hi.astype(F32), jnp.where(lane == 1, square_lo.astype(F32), 0.0))
    rows_z[z, :, COLS:] = spare.astype(BF16)

    def d_copy(j):
        return remote(rows_z.at[z], rows_z.at[z], d_s.at[j], d_r.at[j], dp, zpeer(j))

    for j in range(1, 4):
        d_copy(j).start()
    for j in range(1, 4):
        remote(rows_z.at[zpeer(j)], rows_z.at[zpeer(4 - j)], d_s.at[j], d_r.at[j], dp, zpeer(j)).wait_recv()

    def e_copy(k):
        return remote(x_out.at[k], x_in.at[dp], e_s.at[k], e_r.at[k], peer(k) * 2 + core, z)

    def e2_copy(k):
        which = source(k) * 2 + core
        return remote(x_in.at[which], x_in.at[which], e2_s.at[k], e2_r.at[k], sib, z)

    all_rows = rows_z[...].reshape(TOKENS, WIDE)

    def e_start(k, _):
        x_out[k] = mm(pick[peer(k)], all_rows).astype(BF16)
        e_copy(k).start()
        return 0

    lax.fori_loop(1, XY, e_start, 0)
    x_in[dp] = mm(pick[xy], all_rows).astype(BF16)
    e2_copy(0).start()
    loads[4].wait()

    gate_s[...] = jnp.zeros_like(gate_s)
    up_s[...] = jnp.zeros_like(up_s)
    sq_s[...] = jnp.zeros_like(sq_s)

    def take(which):
        x = x_in[which]
        at = pl.ds(pl.multiple_of(which * COLS, COLS), COLS)
        gate_s[...] += mm(x[:, :COLS], gu_v[0, at, :])
        up_s[...] += mm(x[:, :COLS], gu_v[1, at, :])
        sq_s[...] += x[:, 128:].astype(F32)

    take(dp)

    def e_take(k, _):
        e_copy(k).wait_recv()
        e2_copy(k).start()
        take(source(k) * 2 + core)
        return 0

    lax.fori_loop(1, XY, e_take, 0)

    def e2_take(k, _):
        e2_copy(k).wait_recv()
        take(source(k) * 2 + 1 - core)
        return 0

    lax.fori_loop(0, XY, e2_take, 0)
    square = sq_s[:, COLS - 128 : COLS - 127] + sq_s[:, COLS - 127 : COLS - 126]
    factor = lax.rsqrt(square / D + EPSILON)
    g = gate_s[...] * factor
    u = up_s[...] * factor
    act_s[...] = (g / (1.0 + jnp.exp(-g)) * u).astype(BF16)
    loads[5].wait()
    weight = wcol[:, :1]

    def g_copy(t):
        return remote(y_mine.at[t, 1 - core], y_sib.at[t], g_s.at[t], g_r.at[t], sib, z)

    def results(n, _):
        group = ((xy + 1) // 2 + n) % 8
        at = pl.ds(pl.multiple_of(group * 4 * COLS, 128), 4 * COLS)
        y = mm(act_s[...], down_v[:, at]) * weight
        for k in range(4):
            y_mine[group * 2 + k // 2, k % 2, :, :COLS] = y[:, COLS * k : COLS * (k + 1)].astype(BF16)
        g_copy(group * 2).start()
        g_copy(group * 2 + 1).start()
        return 0

    def blank(n, _):
        for k in range(2):
            y_mine[n, k, :, 128:] = jnp.zeros((ROWS, 128), BF16)
        return 0

    lax.fori_loop(0, XY, blank, 0)
    lax.fori_loop(0, 8, results, 0)

    def g2_copy(k):
        return remote(y_out.at[k], y_in.at[xy], g2_s.at[k], g2_r.at[k], peer(k) * 2 + core, z)

    def both(t):
        g_copy(t).wait_recv()
        return (y_mine[t, core].astype(F32) + y_sib[t].astype(F32)).astype(BF16)

    def g2_start(k, _):
        y_out[k] = both(peer(k))
        g2_copy(k).start()
        return 0

    lax.fori_loop(1, XY, g2_start, 0)
    total = mm(pick_t[xy], both(xy))

    def combine(k, total):
        from_xy = source(k)
        remote(y_out.at[k], y_in.at[from_xy], g2_s.at[k], g2_r.at[k], peer(k) * 2 + core, z).wait_recv()
        return total + mm(pick_t[from_xy], y_in[from_xy])

    total = lax.fori_loop(1, XY, combine, total)
    for q in range(4):
        fin[q] = total[QTOK * q : QTOK * (q + 1)]

    def h_copy(j):
        return remote(fin.at[zpeer(j)], fin_in.at[z], h_s.at[j], h_r.at[j], dp, zpeer(j))

    for j in range(1, 4):
        h_copy(j).start()
    result = fin[z][:, :COLS] + mid_s[...]
    for j in range(1, 4):
        remote(fin.at[zpeer(j)], fin_in.at[zpeer(4 - j)], h_s.at[j], h_r.at[j], dp, zpeer(j)).wait_recv()
        result = result + fin_in[zpeer(4 - j)][:, :COLS]
    out[...] = result.astype(BF16)

    def sent(k, _):
        a_copy(k).wait_send()
        e_copy(k).wait_send()
        g2_copy(k).wait_send()
        return 0

    def sent_sib(k, _):
        a2_copy(k).wait_send()
        e2_copy(k).wait_send()
        g_copy(k).wait_send()
        return 0

    lax.fori_loop(1, XY, sent, 0)
    lax.fori_loop(0, XY, sent_sib, 0)
    for j in range(1, 4):
        c_copy(j).wait_send()
        d_copy(j).wait_send()
        h_copy(j).wait_send()


def on_device(
    query, new_latent, cache, cache_len, w_uv, w_out, hidden_in, norm_gain, routing, route_weight,
    w_gate_up, w_down,
):
    vmem = pl.BlockSpec(memory_space=pltpu.VMEM)
    smem = pl.BlockSpec(memory_space=pltpu.SMEM)
    hbm = pl.BlockSpec(memory_space=pl.ANY)
    dma = pltpu.SemaphoreType.DMA
    return pl.pallas_call(
        kernel,
        out_shape=jax.ShapeDtypeStruct((QTOK, COLS), BF16),
        in_specs=[vmem, vmem, hbm, smem, hbm, hbm, vmem, vmem, vmem, vmem, hbm, hbm],
        out_specs=vmem,
        scratch_shapes=[
            pltpu.VMEM((2, MAXLEN, LAT), BF16),
            pltpu.VMEM((16, KVL, VH), BF16),
            pltpu.VMEM((16 * VH, COLS), BF16),
            pltpu.VMEM((2, D, UNITS), BF16),
            pltpu.VMEM((UNITS, D), BF16),
            pltpu.VMEM((32, 64, VH), BF16),
            pltpu.VMEM((32 * 64, VH), F32),
            pltpu.VMEM((4, QTOK, WIDE), F32),
            pltpu.VMEM((4, QTOK, WIDE), F32),
            pltpu.VMEM((4, QTOK, WIDE), BF16),
            pltpu.VMEM((EXPERTS, ROWS, TOKENS), BF16),
            pltpu.VMEM((EXPERTS, TOKENS, ROWS), BF16),
            pltpu.VMEM((EXPERTS, TOKENS), F32),
            pltpu.VMEM((EXPERTS, TOKENS), F32),
            pltpu.VMEM((QTOK, COLS), F32),
            pltpu.VMEM((ROWS, 128), F32),
            pltpu.VMEM((XY, ROWS, WIDE), BF16),
            pltpu.VMEM((32, ROWS, WIDE), BF16),
            pltpu.VMEM((ROWS, UNITS), F32),
            pltpu.VMEM((ROWS, UNITS), F32),
            pltpu.VMEM((ROWS, 128), F32),
            pltpu.VMEM((ROWS, UNITS), BF16),
            pltpu.VMEM((XY, 2, ROWS, WIDE), BF16),
            pltpu.VMEM((XY, ROWS, WIDE), BF16),
            pltpu.VMEM((XY, ROWS, WIDE), BF16),
            pltpu.VMEM((XY, ROWS, WIDE), BF16),
            pltpu.VMEM((4, QTOK, WIDE), F32),
            pltpu.VMEM((4, QTOK, WIDE), F32),
            dma((6,)),
            dma((XY,)), dma((XY,)), dma((XY,)), dma((XY,)),
            dma((4,)), dma((4,)), dma((4,)), dma((4,)),
            dma((XY,)), dma((XY,)), dma((XY,)), dma((XY,)),
            dma((XY,)), dma((XY,)), dma((XY,)), dma((XY,)),
            dma((4,)), dma((4,)),
        ],
        compiler_params=pltpu.CompilerParams(
            collective_id=0, has_side_effects=True, vmem_limit_bytes=56 * 2**20
        ),
    )(
        query, new_latent, cache, cache_len, w_uv, w_out, hidden_in, norm_gain.reshape(1, COLS),
        routing, route_weight, w_gate_up, w_down,
    )


def solution(mesh):
    placed = (
        P("dp", "tp", None),
        P("dp", None),
        P("dp", None, None),
        P("dp"),
        P("tp", None, None),
        P("tp", "dp"),
        P("tp", "dp"),
        P("dp"),
        P(),
        P(),
        P(None, None, ("dp", "tp")),
        P(("dp", "tp"), None),
    )
    return jax.shard_map(
        on_device, mesh=mesh, in_specs=placed, out_specs=P("tp", "dp"), check_vma=False
    )
```

```python
import jax
import jax.numpy as jnp
from jax import lax
from jax.experimental import pallas as pl
from jax.experimental.pallas import tpu as pltpu
from jax.sharding import PartitionSpec as P

D = 7168
LAT = 576
KVL = 512
ROPE = 64
VH = 128
MAXLEN = 1024
EXPERTS = 16
TOKENS = 128
TOP = 8
QTOK = 32
CAP = 24
ROWS = 4 * CAP
COLS = 224
WIDE = 256
UNITS = 256
XY = 16
HALF = D // 2
EPSILON = 1e-06
MESH = pl.DeviceIdType.MESH
F32 = jnp.float32
BF16 = jnp.bfloat16


def mm(a, b, dims=((1,), (0,)), precision=None):
    return lax.dot_general(a, b, (dims, ((), ())), preferred_element_type=F32, precision=precision)


OFFSETS = [(0, 0)] + sorted(
    [(a, b) for a in range(4) for b in range(4) if (a, b) != (0, 0)],
    key=lambda o: -(min(o[0], 4 - o[0]) + min(o[1], 4 - o[1])),
)


def kernel(
    query, new_latent, cache, cache_len, w_uv, w_out, hidden_in, gain, routing, route_weight,
    w_gate_up, w_down, out,
    cache_v, uv_v, out_v, gu_v, down_v,
    heads, heads32, part, part_in, hidden, pick, mem_t, pos_t, mid_s, wcol, merge,
    x_out, x_a, x_b, gate_s, up_s, sq_s, act_s, y_out, y_in,
    load_sem, hid_s, hid_r, w_s, w_r, a_s, a_r, a2_s, a2_r, c_s, c_r, e_s, e_r, e2_s, e2_r,
    f_s, f_r, g_s, g_r, g_own,
):
    dp = lax.axis_index("dp")
    z = lax.axis_index("tp")
    xy = dp // 2
    core = dp % 2
    sib = xy * 2 + (1 - core)
    side = dp // 16

    def peer(k):
        return (xy // 4 + OFFSETS[k][0]) % 4 * 4 + (xy + OFFSETS[k][1]) % 4

    def source(k):
        return (xy // 4 + 4 - OFFSETS[k][0]) % 4 * 4 + (xy + 4 - OFFSETS[k][1]) % 4

    def zpeer(j):
        return (z + j) % 4

    def remote(src, dst, send, recv, to_dp, to_z):
        return pltpu.make_async_remote_copy(
            src_ref=src, dst_ref=dst, send_sem=send, recv_sem=recv,
            device_id=(to_dp, to_z), device_id_type=MESH,
        )

    barrier = pltpu.get_barrier_semaphore()
    pl.semaphore_signal(barrier, inc=1, device_id=(sib, z), device_id_type=MESH)
    for k in range(1, XY):
        pl.semaphore_signal(barrier, inc=1, device_id=(peer(k) * 2 + core, z), device_id_type=MESH)
    for j in range(1, 4):
        pl.semaphore_signal(barrier, inc=1, device_id=(dp, zpeer(j)), device_id_type=MESH)

    half = pl.ds(pl.multiple_of(core * HALF, 128), HALF)
    other_half = pl.ds(pl.multiple_of((1 - core) * HALF, 128), HALF)
    loads = [
        pltpu.make_async_copy(cache.at[0], cache_v.at[0], load_sem.at[0]),
        pltpu.make_async_copy(cache.at[1], cache_v.at[1], load_sem.at[1]),
        pltpu.make_async_copy(w_uv, uv_v, load_sem.at[2]),
        pltpu.make_async_copy(w_out, out_v, load_sem.at[3]),
        pltpu.make_async_copy(w_gate_up, gu_v, load_sem.at[4]),
        pltpu.make_async_copy(w_down.at[:, half], down_v.at[core], load_sem.at[5]),
    ]
    for copy in loads:
        copy.start()
    hidden[z, :, :COLS] = hidden_in[...]
    hidden[z, :, COLS:] = jnp.zeros((QTOK, WIDE - COLS), BF16)

    scale = float(VH + ROPE) ** (-0.5)
    q_all = query[...].reshape(4 * XY, LAT)
    fresh = new_latent[...]
    near = mm(q_all, fresh, ((1,), (1,))) * scale
    row = lax.broadcasted_iota(jnp.int32, (64, 4), 0)
    col = lax.broadcasted_iota(jnp.int32, (64, 4), 1)
    near = jnp.where((row // 32 == col // 2) & (row // 16 >= col), near, -jnp.inf)
    contexts = []
    for b in range(2):
        loads[b].wait()
        q = q_all[32 * b : 32 * b + 32]
        far = mm(q, cache_v[b]) * scale
        place = lax.broadcasted_iota(jnp.int32, (32, MAXLEN), 1)
        far = jnp.where(place < cache_len[b], far, -jnp.inf)
        close = near[32 * b : 32 * b + 32]
        highest = jnp.maximum(
            jnp.max(far, axis=1, keepdims=True), jnp.max(close, axis=1, keepdims=True)
        )
        far = jnp.exp(far - highest)
        close = jnp.exp(close - highest)
        total = jnp.sum(far, axis=1, keepdims=True) + jnp.sum(close, axis=1, keepdims=True)
        context = mm((far / total).astype(BF16), cache_v[b, :KVL, :], ((1,), (1,)))
        context = context + mm((close / total).astype(BF16), fresh[:, :KVL])
        contexts.append(context.astype(BF16))
    context = jnp.concatenate(contexts, axis=0)
    loads[2].wait()
    row = lax.broadcasted_iota(jnp.int32, (64, VH), 0)
    head_out = jnp.zeros((64, VH), F32)
    for h in range(16):
        head_out = jnp.where(row % 16 == h, mm(context, uv_v[h]), head_out)
    heads[dp] = head_out.astype(BF16)

    pl.semaphore_wait(barrier, XY + 3)

    def a_copy(k):
        return remote(heads.at[dp], heads.at[dp], a_s, a_r.at[k], peer(k) * 2 + core, z)

    def a2_copy(k):
        which = source(k) * 2 + core
        return remote(heads.at[which], heads.at[which], a2_s, a2_r, sib, z)

    for k in range(1, XY):
        a_copy(k).start()
    a2_copy(0).start()

    def hid_copy(j):
        return remote(hidden.at[z], hidden.at[z], hid_s, hid_r, dp, zpeer(j))

    for j in range(1, 4):
        hid_copy(j).start()
    w_copy = remote(w_down.at[:, other_half], down_v.at[core], w_s, w_r, sib, z)
    w_copy.start()

    expert = lax.broadcasted_iota(jnp.int32, (EXPERTS, TOKENS), 0)
    member = jnp.zeros((EXPERTS, TOKENS), F32)
    share = jnp.zeros((1, TOKENS), F32)
    for k in range(TOP):
        named = routing[k : k + 1, :]
        member = member + jnp.where(named == expert, 1.0, 0.0)
        share = share + jnp.where(named == xy, route_weight[k : k + 1, :], 0.0)
    i0 = lax.broadcasted_iota(jnp.int32, (TOKENS, TOKENS), 0)
    i1 = lax.broadcasted_iota(jnp.int32, (TOKENS, TOKENS), 1)
    earlier = jnp.where((i0 < i1) & (i0 // QTOK == i1 // QTOK), 1.0, 0.0).astype(BF16)
    position = mm(member.astype(BF16), earlier)
    mem_t[...] = member
    pos_t[...] = position
    slot = lax.broadcasted_iota(jnp.int32, (ROWS, TOKENS), 0)
    token = lax.broadcasted_iota(jnp.int32, (ROWS, TOKENS), 1)
    in_block = slot // CAP == token // QTOK
    rank = (slot % CAP).astype(F32)
    for k in range(XY):
        e = pl.ds(peer(k), 1)
        here = (mem_t[e, :] > 0.5) & in_block & (pos_t[e, :] == rank)
        pick[k] = jnp.where(here, 1.0, 0.0).astype(BF16)
    weight = jnp.sum(pick[0].astype(F32) * share, axis=1, keepdims=True)
    wcol[...] = jnp.broadcast_to(weight, (ROWS, 128))
    i0 = lax.broadcasted_iota(jnp.int32, (TOKENS, QTOK), 0)
    i1 = lax.broadcasted_iota(jnp.int32, (TOKENS, QTOK), 1)
    own = jnp.where(i0 == i1 + z * QTOK, 1.0, 0.0).astype(BF16)
    spread_e = lax.broadcasted_iota(jnp.int32, (EXPERTS, EXPERTS * 2 * CAP), 0)
    spread_c = lax.broadcasted_iota(jnp.int32, (EXPERTS, EXPERTS * 2 * CAP), 1)
    spread = jnp.where(spread_c // (2 * CAP) == spread_e, 1.0, 0.0).astype(BF16)
    mem_own = mm(mm(member.astype(BF16), own).astype(BF16), spread, ((0,), (0,)))
    pos_own = mm(mm(position.astype(BF16), own).astype(BF16), spread, ((0,), (0,)))
    place = lax.broadcasted_iota(jnp.int32, (QTOK, EXPERTS * 2 * CAP), 1)
    found = (mem_own > 0.5) & (pos_own == (place % CAP).astype(F32))
    first = place % (2 * CAP) < CAP
    merge[:QTOK, :] = jnp.where(found & first, 1.0, 0.0).astype(BF16)
    merge[QTOK:, :] = jnp.where(found & (place % (2 * CAP) >= CAP), 1.0, 0.0).astype(BF16)

    for k in range(1, XY):
        a_copy(k).wait_recv()
        a2_copy(k).start()
    remote(heads.at[pl.ds(0, XY)], heads.at[pl.ds(0, XY)], a2_s, a2_r, sib, z).wait_recv()
    heads32[...] = heads[...].reshape(32 * 64, VH).astype(F32)
    loads[3].wait()
    projected = jnp.zeros((TOKENS, COLS), F32)
    for h in range(0, 16, 2):
        lhs = jnp.concatenate(
            [heads32[pl.ds(h, TOKENS, stride=16), :], heads32[pl.ds(h + 1, TOKENS, stride=16), :]], axis=1
        ).astype(BF16)
        projected = projected + mm(lhs, out_v[:, VH * h : VH * (h + 2)], ((1,), (1,)))
    part[:, :COLS] = projected.astype(BF16)
    part[:, COLS:] = jnp.zeros((TOKENS, WIDE - COLS), BF16)

    def c_copy(j):
        return remote(part, part_in.at[j], c_s, c_r.at[j], dp, zpeer(j))

    for j in range(1, 4):
        c_copy(j).start()
    remote(hidden.at[pl.ds(0, 3)], hidden.at[pl.ds(0, 3)], hid_s, hid_r, dp, zpeer(1)).wait_recv()
    mid = projected + hidden[...].reshape(TOKENS, WIDE)[:, :COLS].astype(F32)
    for j in (1, 3, 2):
        c_copy(j).wait_recv()
        mid = mid + part_in[j][:, :COLS].astype(F32)
    mid_s[...] = mid
    square = jnp.sum(mid * mid, axis=1, keepdims=True)
    square_hi = square.astype(BF16).astype(F32)
    square_lo = square - square_hi
    lane = lax.broadcasted_iota(jnp.int32, (TOKENS, WIDE - COLS), 1)
    spare = jnp.where(lane == 0, square_hi, jnp.where(lane == 1, square_lo, 0.0))
    all_rows = jnp.concatenate([(mid * gain[...]), spare], axis=1).astype(BF16)
    def e_copy(k):
        return remote(x_out.at[k], x_a.at[k], e_s, e_r.at[k], peer(k) * 2 + core, z)

    def e2_copy(k):
        return remote(x_a.at[k], x_b.at[k], e2_s, e2_r.at[k], sib, z)

    for first in range(1, XY, 5):
        rows = mm(pick[first : first + 5].reshape(5 * ROWS, TOKENS), all_rows).astype(BF16)
        for k in range(first, first + 5):
            x_out[k] = rows[ROWS * (k - first) : ROWS * (k - first + 1)]
            e_copy(k).start()
    x_a[0] = mm(pick[0], all_rows).astype(BF16)
    e2_copy(0).start()
    loads[4].wait()

    def take(buffer, ks, owner, start=False):
        gate, up, squares = (0.0, 0.0, 0.0) if start else (gate_s[...], up_s[...], sq_s[...])
        for k in ks:
            x = buffer[k]
            at = pl.ds(pl.multiple_of((source(k) * 2 + owner) * COLS, 32), COLS)
            gate = gate + mm(x[:, :COLS], gu_v[0, at, :])
            up = up + mm(x[:, :COLS], gu_v[1, at, :])
            squares = squares + x[:, 128:].astype(F32)
        gate_s[...] = gate
        up_s[...] = up
        sq_s[...] = squares

    def plane(ks):
        for k in ks:
            e_copy(k).wait_recv()
            e2_copy(k).start()

    def sibling(ks):
        for k in ks:
            e2_copy(k).wait_recv()

    take(x_a, [0], core, True)
    plane(range(1, 6))
    take(x_a, range(1, 6), core)
    plane(range(6, 11))
    sibling(range(0, 6))
    take(x_a, range(6, 11), core)
    take(x_b, range(0, 6), 1 - core)
    plane(range(11, 16))
    sibling(range(6, 11))
    take(x_b, range(6, 11), 1 - core)
    take(x_a, range(11, 16), core)
    sibling(range(11, 16))
    take(x_b, range(11, 16), 1 - core)
    square = sq_s[:, COLS - 128 : COLS - 127] + sq_s[:, COLS - 127 : COLS - 126]
    factor = lax.rsqrt(square / D + EPSILON)
    g = gate_s[...] * factor
    u = up_s[...] * factor
    act_s[core] = (g / (1.0 + jnp.exp(-g)) * u).astype(BF16)
    f_copy = remote(act_s.at[core], act_s.at[core], f_s, f_r, sib, z)
    f_copy.start()
    loads[5].wait()
    w_copy.wait_recv()
    f_copy.wait_recv()
    weight = wcol[:, :1]

    def g_copy(m, q):
        return remote(y_out.at[m, q], y_in.at[z * XY + xy], g_s, g_r, core * 16 + m, q)

    def g_self(m, q):
        return pltpu.make_async_copy(y_out.at[m, q], y_in.at[z * XY + xy], g_own)

    def results(n, _):
        group = (dp // 4 % 4 + n) % 4
        at = pl.ds(pl.multiple_of(group * 4 * COLS, 128), 4 * COLS)
        y = (mm(act_s[0], down_v[0, :, at]) + mm(act_s[1], down_v[1, :, at])) * weight
        for k in range(4):
            low = y[:, COLS * k : COLS * k + 128]
            high = jnp.concatenate(
                [y[:, COLS * k + 128 : COLS * (k + 1)], jnp.zeros((ROWS, WIDE - COLS), F32)], axis=1
            )
            m = group * 4 + k
            for q in range(4):
                at_q = slice(CAP * q, CAP * (q + 1))
                y_out[m, q] = jnp.concatenate([low[at_q], high[at_q]], axis=0).astype(BF16)
                to_self = (core * 16 + m == dp) & (z == q)

                @pl.when(to_self)
                def _():
                    g_self(m, q).start()

                @pl.when(jnp.logical_not(to_self))
                def _():
                    g_copy(m, q).start()

        return 0

    lax.fori_loop(0, 4, results, 0)
    mine = side == core

    def slabs(count):
        return remote(y_in.at[pl.ds(0, count)], y_in.at[pl.ds(0, count)], g_s, g_r, sib, z)

    @pl.when(mine)
    def _():
        slabs(63).wait_recv()
        g_self(0, 0).wait()

    @pl.when(jnp.logical_not(mine))
    def _():
        slabs(64).wait_recv()

    total = jnp.zeros((2 * QTOK, 128), F32)
    for j in range(4):
        total = total + mm(merge[...], y_in[XY * j : XY * (j + 1)].reshape(XY * 2 * CAP, 128))
    total = jnp.concatenate([total[:QTOK], total[QTOK:, : COLS - 128]], axis=1)
    out[...] = (mid_s[pl.ds(pl.multiple_of(z * QTOK, QTOK), QTOK), :] + total).astype(BF16)

    def left(ref, sem):
        remote(ref, ref, sem, w_r, sib, z).wait_send()

    left(heads.at[pl.ds(0, 15)], a_s)
    left(heads.at[pl.ds(0, 16)], a2_s)
    left(hidden.at[pl.ds(0, 3)], hid_s)
    w_copy.wait_send()
    left(part_in.at[pl.ds(0, 3)], c_s)
    left(x_out.at[pl.ds(0, 15)], e_s)
    left(x_a, e2_s)
    f_copy.wait_send()

    @pl.when(mine)
    def _():
        slabs(63).wait_send()

    @pl.when(jnp.logical_not(mine))
    def _():
        slabs(64).wait_send()


def on_device(
    query, new_latent, cache, cache_len, w_uv, w_out, hidden_in, norm_gain, routing, route_weight,
    w_gate_up, w_down,
):
    vmem = pl.BlockSpec(memory_space=pltpu.VMEM)
    smem = pl.BlockSpec(memory_space=pltpu.SMEM)
    hbm = pl.BlockSpec(memory_space=pl.ANY)
    dma = pltpu.SemaphoreType.DMA
    return pl.pallas_call(
        kernel,
        out_shape=jax.ShapeDtypeStruct((QTOK, COLS), BF16),
        in_specs=[vmem, vmem, hbm, smem, hbm, hbm, vmem, vmem, vmem, vmem, hbm, hbm],
        out_specs=vmem,
        scratch_shapes=[
            pltpu.VMEM((2, LAT, MAXLEN), BF16),
            pltpu.VMEM((16, KVL, VH), BF16),
            pltpu.VMEM((COLS, 16 * VH), BF16),
            pltpu.VMEM((2, D, UNITS), BF16),
            pltpu.VMEM((2, UNITS, HALF), BF16),
            pltpu.VMEM((32, 64, VH), BF16),
            pltpu.VMEM((32 * 64, VH), F32),
            pltpu.VMEM((TOKENS, WIDE), BF16),
            pltpu.VMEM((4, TOKENS, WIDE), BF16),
            pltpu.VMEM((4, QTOK, WIDE), BF16),
            pltpu.VMEM((XY, ROWS, TOKENS), BF16),
            pltpu.VMEM((EXPERTS, TOKENS), F32),
            pltpu.VMEM((EXPERTS, TOKENS), F32),
            pltpu.VMEM((TOKENS, COLS), F32),
            pltpu.VMEM((ROWS, 128), F32),
            pltpu.VMEM((2 * QTOK, XY * 2 * CAP), BF16),
            pltpu.VMEM((XY, ROWS, WIDE), BF16),
            pltpu.VMEM((XY, ROWS, WIDE), BF16),
            pltpu.VMEM((XY, ROWS, WIDE), BF16),
            pltpu.VMEM((ROWS, UNITS), F32),
            pltpu.VMEM((ROWS, UNITS), F32),
            pltpu.VMEM((ROWS, 128), F32),
            pltpu.VMEM((2, ROWS, UNITS), BF16),
            pltpu.VMEM((XY, 4, 2 * CAP, 128), BF16),
            pltpu.VMEM((4 * XY, 2 * CAP, 128), BF16),
            dma((6,)),
            dma, dma, dma, dma,
            dma, dma((XY,)), dma, dma,
            dma, dma((4,)),
            dma, dma((XY,)), dma, dma((XY,)),
            dma, dma, dma, dma, dma,
        ],
        compiler_params=pltpu.CompilerParams(
            collective_id=0, has_side_effects=True, vmem_limit_bytes=56 * 2**20
        ),
    )(
        query, new_latent, cache.transpose(0, 2, 1), cache_len, w_uv, w_out.T, hidden_in,
        norm_gain.reshape(1, COLS), routing.T, route_weight.T, w_gate_up, w_down,
    )


def solution(mesh):
    placed = (
        P("dp", "tp", None),
        P("dp", None),
        P("dp", None, None),
        P("dp"),
        P("tp", None, None),
        P("tp", "dp"),
        P("tp", "dp"),
        P("dp"),
        P(),
        P(),
        P(None, None, ("dp", "tp")),
        P(("dp", "tp"), None),
    )
    return jax.shard_map(
        on_device, mesh=mesh, in_specs=placed, out_specs=P("tp", "dp"), check_vma=False
    )
```

```python
import jax
import jax.numpy as jnp
from jax import lax
from jax.experimental import pallas as pl
from jax.experimental.pallas import tpu as pltpu
from jax.sharding import PartitionSpec as P

D = 7168
LAT = 576
KVL = 512
ROPE = 64
VH = 128
MAXLEN = 1024
EXPERTS = 16
TOKENS = 128
TOP = 8
QTOK = 32
CAP = 24
ROWS = 4 * CAP
COLS = 224
WIDE = 256
UNITS = 256
XY = 16
HALF = D // 2
PART = ROWS // 2
EPSILON = 1e-06
MESH = pl.DeviceIdType.MESH
F32 = jnp.float32
BF16 = jnp.bfloat16


def mm(a, b, dims=((1,), (0,)), precision=None):
    return lax.dot_general(a, b, (dims, ((), ())), preferred_element_type=F32, precision=precision)


OFFSETS = [(0, 0)] + sorted(
    [(a, b) for a in range(4) for b in range(4) if (a, b) != (0, 0)],
    key=lambda o: -(min(o[0], 4 - o[0]) + min(o[1], 4 - o[1])),
)


def kernel(
    query, new_latent, cache, cache_len, w_uv, w_out, hidden_in, gain, routing, route_weight,
    w_gate_up, w_down, out,
    cache_v, uv_v, out_v, gu_v, down_v,
    heads_a, heads_b, heads32, part, part_in, hidden, pick, mem_t, pos_t, mid_s, wcol, merge,
    x_out, x_a, x_b, act_s, y_out, y_in,
    load_sem, hid_s, hid_r, w_s, w_r, a_s, a_r, a2_s, a2_r, c_s, c_r, e_s, e_r, e2_s, e2_r,
    f_s, f_r, g_s, g_r, g_own,
):
    dp = lax.axis_index("dp")
    z = lax.axis_index("tp")
    xy = dp // 2
    core = dp % 2
    sib = xy * 2 + (1 - core)
    side = dp // 16

    def peer(k):
        return (xy // 4 + OFFSETS[k][0]) % 4 * 4 + (xy + OFFSETS[k][1]) % 4

    def source(k):
        return (xy // 4 + 4 - OFFSETS[k][0]) % 4 * 4 + (xy + 4 - OFFSETS[k][1]) % 4

    def zpeer(j):
        return (z + j) % 4

    def remote(src, dst, send, recv, to_dp, to_z):
        return pltpu.make_async_remote_copy(
            src_ref=src, dst_ref=dst, send_sem=send, recv_sem=recv,
            device_id=(to_dp, to_z), device_id_type=MESH,
        )

    barrier = pltpu.get_barrier_semaphore()
    pl.semaphore_signal(barrier, inc=1, device_id=(sib, z), device_id_type=MESH)
    for k in range(1, XY):
        pl.semaphore_signal(barrier, inc=1, device_id=(peer(k) * 2 + core, z), device_id_type=MESH)
    for j in range(1, 4):
        pl.semaphore_signal(barrier, inc=1, device_id=(dp, zpeer(j)), device_id_type=MESH)

    half = pl.ds(pl.multiple_of(core * HALF, 128), HALF)
    other_half = pl.ds(pl.multiple_of((1 - core) * HALF, 128), HALF)
    loads = [
        pltpu.make_async_copy(cache.at[0], cache_v.at[0], load_sem.at[0]),
        pltpu.make_async_copy(cache.at[1], cache_v.at[1], load_sem.at[1]),
        pltpu.make_async_copy(w_uv, uv_v, load_sem.at[2]),
        pltpu.make_async_copy(w_out, out_v, load_sem.at[3]),
        pltpu.make_async_copy(w_gate_up, gu_v, load_sem.at[4]),
        pltpu.make_async_copy(w_down.at[:, half], down_v.at[core], load_sem.at[5]),
    ]
    for copy in loads:
        copy.start()
    hidden[z, :, :COLS] = hidden_in[...]
    hidden[z, :, COLS:] = jnp.zeros((QTOK, WIDE - COLS), BF16)

    scale = float(VH + ROPE) ** (-0.5)
    q_all = query[...].reshape(4 * XY, LAT)
    fresh = new_latent[...]
    near = mm(q_all, fresh, ((1,), (1,))) * scale
    row = lax.broadcasted_iota(jnp.int32, (64, 4), 0)
    col = lax.broadcasted_iota(jnp.int32, (64, 4), 1)
    near = jnp.where((row // 32 == col // 2) & (row // 16 >= col), near, -jnp.inf)
    contexts = []
    for b in range(2):
        loads[b].wait()
        q = q_all[32 * b : 32 * b + 32]
        far = mm(q, cache_v[b]) * scale
        place = lax.broadcasted_iota(jnp.int32, (32, MAXLEN), 1)
        far = jnp.where(place < cache_len[b], far, -jnp.inf)
        close = near[32 * b : 32 * b + 32]
        highest = jnp.maximum(
            jnp.max(far, axis=1, keepdims=True), jnp.max(close, axis=1, keepdims=True)
        )
        far = jnp.exp(far - highest)
        close = jnp.exp(close - highest)
        total = jnp.sum(far, axis=1, keepdims=True) + jnp.sum(close, axis=1, keepdims=True)
        context = mm((far / total).astype(BF16), cache_v[b, :KVL, :], ((1,), (1,)))
        context = context + mm((close / total).astype(BF16), fresh[:, :KVL])
        contexts.append(context.astype(BF16))
    context = jnp.concatenate(contexts, axis=0)
    loads[2].wait()
    row = lax.broadcasted_iota(jnp.int32, (64, VH), 0)
    head_out = jnp.zeros((64, VH), F32)
    for h in range(16):
        head_out = jnp.where(row % 16 == h, mm(context, uv_v[h]), head_out)
    heads_a[0] = head_out.astype(BF16)

    pl.semaphore_wait(barrier, XY + 3)

    def a_copy(k):
        return remote(heads_a.at[0], heads_a.at[k], a_s, a_r.at[(k - 1) // 5], peer(k) * 2 + core, z)

    def a2_copy(ks, sem):
        return remote(heads_a.at[ks], heads_b.at[ks], a2_s, sem, sib, z)

    for k in range(1, XY):
        a_copy(k).start()
    a2_copy(pl.ds(0, 1), a2_r.at[3]).start()

    def hid_copy(j):
        return remote(hidden.at[z], hidden.at[z], hid_s, hid_r, dp, zpeer(j))

    for j in range(1, 4):
        hid_copy(j).start()
    w_copy = remote(w_down.at[:, other_half], down_v.at[core], w_s, w_r, sib, z)
    w_copy.start()

    expert = lax.broadcasted_iota(jnp.int32, (EXPERTS, TOKENS), 0)
    member = jnp.zeros((EXPERTS, TOKENS), F32)
    share = jnp.zeros((1, TOKENS), F32)
    for k in range(TOP):
        named = routing[k : k + 1, :]
        member = member + jnp.where(named == expert, 1.0, 0.0)
        share = share + jnp.where(named == xy, route_weight[k : k + 1, :], 0.0)
    i0 = lax.broadcasted_iota(jnp.int32, (TOKENS, TOKENS), 0)
    i1 = lax.broadcasted_iota(jnp.int32, (TOKENS, TOKENS), 1)
    earlier = jnp.where((i0 < i1) & (i0 // QTOK == i1 // QTOK), 1.0, 0.0).astype(BF16)
    position = mm(member.astype(BF16), earlier)
    mem_t[...] = member
    pos_t[...] = position
    slot = lax.broadcasted_iota(jnp.int32, (ROWS, TOKENS), 0)
    token = lax.broadcasted_iota(jnp.int32, (ROWS, TOKENS), 1)
    in_block = slot // CAP == token // QTOK
    rank = (slot % CAP).astype(F32)
    for k in range(XY):
        e = pl.ds(peer(k), 1)
        here = (mem_t[e, :] > 0.5) & in_block & (pos_t[e, :] == rank)
        chosen = jnp.where(here, 1.0, 0.0)
        for h in range(2):
            pick[h, k] = chosen[h * PART : (h + 1) * PART].astype(BF16)
        if k == 0:
            wcol[...] = jnp.broadcast_to(jnp.sum(chosen * share, axis=1, keepdims=True), (ROWS, 128))
    i0 = lax.broadcasted_iota(jnp.int32, (TOKENS, QTOK), 0)
    i1 = lax.broadcasted_iota(jnp.int32, (TOKENS, QTOK), 1)
    own = jnp.where(i0 == i1 + z * QTOK, 1.0, 0.0).astype(BF16)
    spread_e = lax.broadcasted_iota(jnp.int32, (EXPERTS, EXPERTS * 2 * CAP), 0)
    spread_c = lax.broadcasted_iota(jnp.int32, (EXPERTS, EXPERTS * 2 * CAP), 1)
    spread = jnp.where(spread_c // (2 * CAP) == spread_e, 1.0, 0.0).astype(BF16)
    mem_own = mm(mm(member.astype(BF16), own).astype(BF16), spread, ((0,), (0,)))
    pos_own = mm(mm(position.astype(BF16), own).astype(BF16), spread, ((0,), (0,)))
    place = lax.broadcasted_iota(jnp.int32, (QTOK, EXPERTS * 2 * CAP), 1)
    found = (mem_own > 0.5) & (pos_own == (place % CAP).astype(F32))
    first = place % (2 * CAP) < CAP
    merge[:QTOK, :] = jnp.where(found & first, 1.0, 0.0).astype(BF16)
    merge[QTOK:, :] = jnp.where(found & (place % (2 * CAP) >= CAP), 1.0, 0.0).astype(BF16)

    def groups(buffer, sem):
        return remote(buffer, buffer, a_s, sem, sib, z)

    fives = [pl.ds(5 * g + 1, 5) for g in range(3)]

    def spread_heads(buffer, owner, ks):
        for k in ks:
            at = pl.multiple_of((source(k) * 2 + owner) * 64, 64)
            heads32[pl.ds(at, 64), :] = buffer[k].astype(F32)

    spread_heads(heads_a, core, [0])
    for g in range(3):
        groups(heads_a.at[fives[g]], a_r.at[g]).wait_recv()
        a2_copy(fives[g], a2_r.at[g]).start()
        spread_heads(heads_a, core, range(5 * g + 1, 5 * g + 6))
    a2_copy(pl.ds(0, 1), a2_r.at[3]).wait_recv()
    spread_heads(heads_b, 1 - core, [0])
    for g in range(3):
        a2_copy(fives[g], a2_r.at[g]).wait_recv()
        spread_heads(heads_b, 1 - core, range(5 * g + 1, 5 * g + 6))
    loads[3].wait()
    projected = jnp.zeros((TOKENS, COLS), F32)
    for h in range(0, 16, 2):
        lhs = jnp.concatenate(
            [heads32[pl.ds(h, TOKENS, stride=16), :], heads32[pl.ds(h + 1, TOKENS, stride=16), :]], axis=1
        ).astype(BF16)
        projected = projected + mm(lhs, out_v[:, VH * h : VH * (h + 2)], ((1,), (1,)))
    part[:, :COLS] = projected.astype(BF16)
    part[:, COLS:] = jnp.zeros((TOKENS, WIDE - COLS), BF16)

    def c_copy(j):
        return remote(part, part_in.at[j], c_s, c_r.at[j], dp, zpeer(j))

    for j in range(1, 4):
        c_copy(j).start()
    remote(hidden.at[pl.ds(0, 3)], hidden.at[pl.ds(0, 3)], hid_s, hid_r, dp, zpeer(1)).wait_recv()
    mid = projected + hidden[...].reshape(TOKENS, WIDE)[:, :COLS].astype(F32)
    for j in (1, 3, 2):
        c_copy(j).wait_recv()
        mid = mid + part_in[j][:, :COLS].astype(F32)
    mid_s[...] = mid
    square = jnp.sum(mid * mid, axis=1, keepdims=True)
    square_hi = square.astype(BF16).astype(F32)
    square_lo = square - square_hi
    lane = lax.broadcasted_iota(jnp.int32, (TOKENS, WIDE - COLS), 1)
    spare = jnp.where(lane == 0, square_hi, jnp.where(lane == 1, square_lo, 0.0))
    all_rows = jnp.concatenate([(mid * gain[...]), spare], axis=1).astype(BF16)
    def e_copy(h, k):
        return remote(
            x_out.at[h, k], x_a.at[h, k], e_s, e_r.at[h * 3 + (k - 1) // 5], peer(k) * 2 + core, z
        )

    def e2_copy(h, ks, n):
        return remote(x_a.at[h, ks], x_b.at[h, ks], e2_s, e2_r.at[h * 4 + n], sib, z)

    for h in range(2):
        for first in range(1, XY, 5):
            rows = mm(pick[h, first : first + 5].reshape(5 * PART, TOKENS), all_rows).astype(BF16)
            for k in range(first, first + 5):
                x_out[h, k] = rows[PART * (k - first) : PART * (k - first + 1)]
                e_copy(h, k).start()
        x_a[h, 0] = mm(pick[h, 0], all_rows).astype(BF16)
        e2_copy(h, pl.ds(0, 1), 3).start()
    loads[4].wait()

    def take(sums, buffer, h, ks, owner):
        gate, up, squares = sums
        for k in ks:
            x = buffer[h, k]
            at = pl.ds(pl.multiple_of((source(k) * 2 + owner) * COLS, 32), COLS)
            gate = gate + mm(x[:, :COLS], gu_v[0, at, :])
            up = up + mm(x[:, :COLS], gu_v[1, at, :])
            squares = squares + x[:, 128:].astype(F32)
        return gate, up, squares

    def arrive(h, g):
        groups(x_a.at[h, fives[g]], e_r.at[h * 3 + g]).wait_recv()
        e2_copy(h, fives[g], g).start()

    def take_a(sums, h, g):
        return take(sums, x_a, h, range(5 * g + 1, 5 * g + 6), core)

    def take_b(sums, h, g):
        e2_copy(h, fives[g], g).wait_recv()
        return take(sums, x_b, h, range(5 * g + 1, 5 * g + 6), 1 - core)

    def take_own(h):
        sums = (jnp.zeros((PART, UNITS), F32), jnp.zeros((PART, UNITS), F32), jnp.zeros((PART, 128), F32))
        sums = take(sums, x_a, h, [0], core)
        e2_copy(h, pl.ds(0, 1), 3).wait_recv()
        return take(sums, x_b, h, [0], 1 - core)

    def f_copy(h):
        return remote(act_s.at[core, h], act_s.at[core, h], f_s.at[h], f_r.at[h], sib, z)

    def activate(sums, h):
        gate, up, squares = sums
        square = squares[:, COLS - 128 : COLS - 127] + squares[:, COLS - 127 : COLS - 126]
        factor = lax.rsqrt(square / D + EPSILON)
        g = gate * factor
        u = up * factor
        act_s[core, h] = (g / (1.0 + jnp.exp(-g)) * u).astype(BF16)
        f_copy(h).start()

    def g_copy(m, q):
        return remote(y_out.at[m, q], y_in.at[z * XY + xy], g_s, g_r, core * 16 + m, q)

    def g_self(m, q):
        return pltpu.make_async_copy(y_out.at[m, q], y_in.at[z * XY + xy], g_own)

    def results(h, n):
        group = (dp // 4 % 4 + n) % 4
        at = pl.ds(pl.multiple_of(group * 4 * COLS, 128), 4 * COLS)
        y = mm(act_s[0, h], down_v[0, :, at]) + mm(act_s[1, h], down_v[1, :, at])
        y = y * wcol[PART * h : PART * (h + 1), :1]
        for k in range(4):
            low = y[:, COLS * k : COLS * k + 128]
            high = jnp.concatenate(
                [y[:, COLS * k + 128 : COLS * (k + 1)], jnp.zeros((PART, WIDE - COLS), F32)], axis=1
            )
            for q in range(2):
                at_q = slice(CAP * q, CAP * (q + 1))
                slab = jnp.concatenate([low[at_q], high[at_q]], axis=0)
                y_out[group * 4 + k, 2 * h + q] = slab.astype(BF16)
        for i in range(4):
            for j in range(2):
                m = group * 4 + (dp + i) % 4
                q = 2 * h + (z + j) % 2
                if n == 0 and i == 0 and j == 0:
                    to_self = (core * 16 + m == dp) & (z == q)

                    @pl.when(to_self)
                    def _():
                        g_self(m, q).start()

                    @pl.when(jnp.logical_not(to_self))
                    def _():
                        g_copy(m, q).start()

                else:
                    g_copy(m, q).start()

    sums = take_own(0)
    for g in range(3):
        arrive(0, g)
        sums = take_a(sums, 0, g)
    for g in range(3):
        sums = take_b(sums, 0, g)
    activate(sums, 0)
    sums = take_own(1)
    arrive(1, 0)
    sums = take_a(sums, 1, 0)
    sums = take_b(sums, 1, 0)
    loads[5].wait()
    w_copy.wait_recv()
    f_copy(0).wait_recv()
    results(0, 0)
    arrive(1, 1)
    results(0, 1)
    results(0, 2)
    arrive(1, 2)
    results(0, 3)
    sums = take_a(sums, 1, 1)
    sums = take_b(sums, 1, 1)
    sums = take_a(sums, 1, 2)
    sums = take_b(sums, 1, 2)
    activate(sums, 1)
    f_copy(1).wait_recv()
    for n in range(4):
        results(1, n)
    mine = side == core

    def slabs(count):
        return remote(y_in.at[pl.ds(0, count)], y_in.at[pl.ds(0, count)], g_s, g_r, sib, z)

    @pl.when(mine)
    def _():
        slabs(63).wait_recv()
        g_self(0, 0).wait()

    @pl.when(jnp.logical_not(mine))
    def _():
        slabs(64).wait_recv()

    total = jnp.zeros((2 * QTOK, 128), F32)
    for j in range(4):
        total = total + mm(merge[...], y_in[XY * j : XY * (j + 1)].reshape(XY * 2 * CAP, 128))
    total = jnp.concatenate([total[:QTOK], total[QTOK:, : COLS - 128]], axis=1)
    out[...] = (mid_s[pl.ds(pl.multiple_of(z * QTOK, QTOK), QTOK), :] + total).astype(BF16)

    def left(ref, sem):
        remote(ref, ref, sem, w_r, sib, z).wait_send()

    left(heads_a.at[pl.ds(0, 15)], a_s)
    left(heads_a, a2_s)
    left(hidden.at[pl.ds(0, 3)], hid_s)
    w_copy.wait_send()
    left(part_in.at[pl.ds(0, 3)], c_s)
    left(x_out.at[0], e_s)
    left(x_out.at[0, pl.ds(0, 14)], e_s)
    left(x_a, e2_s)
    for h in range(2):
        f_copy(h).wait_send()

    @pl.when(mine)
    def _():
        slabs(63).wait_send()

    @pl.when(jnp.logical_not(mine))
    def _():
        slabs(64).wait_send()


def on_device(
    query, new_latent, cache, cache_len, w_uv, w_out, hidden_in, norm_gain, routing, route_weight,
    w_gate_up, w_down,
):
    vmem = pl.BlockSpec(memory_space=pltpu.VMEM)
    smem = pl.BlockSpec(memory_space=pltpu.SMEM)
    hbm = pl.BlockSpec(memory_space=pl.ANY)
    dma = pltpu.SemaphoreType.DMA
    return pl.pallas_call(
        kernel,
        out_shape=jax.ShapeDtypeStruct((QTOK, COLS), BF16),
        in_specs=[vmem, vmem, hbm, smem, hbm, hbm, vmem, vmem, vmem, vmem, hbm, hbm],
        out_specs=vmem,
        scratch_shapes=[
            pltpu.VMEM((2, LAT, MAXLEN), BF16),
            pltpu.VMEM((16, KVL, VH), BF16),
            pltpu.VMEM((COLS, 16 * VH), BF16),
            pltpu.VMEM((2, D, UNITS), BF16),
            pltpu.VMEM((2, UNITS, HALF), BF16),
            pltpu.VMEM((XY, 64, VH), BF16),
            pltpu.VMEM((XY, 64, VH), BF16),
            pltpu.VMEM((32 * 64, VH), F32),
            pltpu.VMEM((TOKENS, WIDE), BF16),
            pltpu.VMEM((4, TOKENS, WIDE), BF16),
            pltpu.VMEM((4, QTOK, WIDE), BF16),
            pltpu.VMEM((2, XY, PART, TOKENS), BF16),
            pltpu.VMEM((EXPERTS, TOKENS), F32),
            pltpu.VMEM((EXPERTS, TOKENS), F32),
            pltpu.VMEM((TOKENS, COLS), F32),
            pltpu.VMEM((ROWS, 128), F32),
            pltpu.VMEM((2 * QTOK, XY * 2 * CAP), BF16),
            pltpu.VMEM((2, XY, PART, WIDE), BF16),
            pltpu.VMEM((2, XY, PART, WIDE), BF16),
            pltpu.VMEM((2, XY, PART, WIDE), BF16),
            pltpu.VMEM((2, 2, PART, UNITS), BF16),
            pltpu.VMEM((XY, 4, 2 * CAP, 128), BF16),
            pltpu.VMEM((4 * XY, 2 * CAP, 128), BF16),
            dma((6,)),
            dma, dma, dma, dma,
            dma, dma((3,)), dma, dma((4,)),
            dma, dma((4,)),
            dma, dma((6,)), dma, dma((8,)),
            dma((2,)), dma((2,)), dma, dma, dma,
        ],
        compiler_params=pltpu.CompilerParams(
            collective_id=0, has_side_effects=True, vmem_limit_bytes=56 * 2**20
        ),
    )(
        query, new_latent, cache.transpose(0, 2, 1), cache_len, w_uv, w_out.T, hidden_in,
        norm_gain.reshape(1, COLS), routing.T, route_weight.T, w_gate_up, w_down,
    )


def solution(mesh):
    placed = (
        P("dp", "tp", None),
        P("dp", None),
        P("dp", None, None),
        P("dp"),
        P("tp", None, None),
        P("tp", "dp"),
        P("tp", "dp"),
        P("dp"),
        P(),
        P(),
        P(None, None, ("dp", "tp")),
        P(("dp", "tp"), None),
    )
    return jax.shard_map(
        on_device, mesh=mesh, in_specs=placed, out_specs=P("tp", "dp"), check_vma=False
    )
```

```python
import jax
import jax.numpy as jnp
from jax import lax
from jax.experimental import pallas as pl
from jax.experimental.pallas import tpu as pltpu
from jax.sharding import PartitionSpec as P

D = 7168
LAT = 576
KVL = 512
ROPE = 64
VH = 128
MAXLEN = 1024
EXPERTS = 16
TOKENS = 128
TOP = 8
QTOK = 32
CAP = 24
ROWS = 4 * CAP
COLS = 224
WIDE = 256
UNITS = 256
XY = 16
HALF = D // 2
PART = ROWS // 2
EPSILON = 1e-06
MESH = pl.DeviceIdType.MESH
F32 = jnp.float32
BF16 = jnp.bfloat16


def mm(a, b, dims=((1,), (0,)), precision=None):
    return lax.dot_general(a, b, (dims, ((), ())), preferred_element_type=F32, precision=precision)


OFFSETS = [(0, 0)] + sorted(
    [(a, b) for a in range(4) for b in range(4) if (a, b) != (0, 0)],
    key=lambda o: -(min(o[0], 4 - o[0]) + min(o[1], 4 - o[1])),
)


def kernel(
    query_h, new_latent_h, cache, cache_len_h, w_uv, w_out, hidden_in_h, gain_h, routing_h,
    route_weight_h, w_gate_up, w_down, out,
    query, new_latent, cache_len, hidden_in, gain, routing, route_weight, cache_v, uv_v, out_v, gu_v, down_v, down_p,
    heads_a, heads_b, heads32, proj, part, part_in, hidden, pick, mem_t, pos_t, mid_s, wcol, merge,
    x_out, x_a, x_b, act_s, y_out, y_in,
    load_sem, hid_s, hid_r, w_s, w_r, a_s, a_r, a2_s, a2_r, c_s, c_r, e_s, e_r, e2_s, e2_r,
    f_s, f_r, g_s, g_r, g_own,
):
    dp = lax.axis_index("dp")
    z = lax.axis_index("tp")
    xy = dp // 2
    core = dp % 2
    sib = xy * 2 + (1 - core)
    side = dp // 16

    def peer(k):
        return (xy // 4 + OFFSETS[k][0]) % 4 * 4 + (xy + OFFSETS[k][1]) % 4

    def source(k):
        return (xy // 4 + 4 - OFFSETS[k][0]) % 4 * 4 + (xy + 4 - OFFSETS[k][1]) % 4

    def zpeer(j):
        return (z + j) % 4

    def remote(src, dst, send, recv, to_dp, to_z):
        return pltpu.make_async_remote_copy(
            src_ref=src, dst_ref=dst, send_sem=send, recv_sem=recv,
            device_id=(to_dp, to_z), device_id_type=MESH,
        )

    barrier = pltpu.get_barrier_semaphore()
    for k in range(1, XY):
        pl.semaphore_signal(barrier, inc=1, device_id=(peer(k) * 2 + core, z), device_id_type=MESH)
    for j in (2, 1, 3):
        pl.semaphore_signal(barrier, inc=1, device_id=(dp, zpeer(j)), device_id_type=MESH)
    pl.semaphore_signal(barrier, inc=1, device_id=(sib, z), device_id_type=MESH)

    half = pl.ds(pl.multiple_of(core * HALF, 128), HALF)
    other_half = pl.ds(pl.multiple_of((1 - core) * HALF, 128), HALF)
    loads = [
        pltpu.make_async_copy(cache.at[0], cache_v.at[0], load_sem.at[0]),
        pltpu.make_async_copy(cache.at[1], cache_v.at[1], load_sem.at[1]),
        pltpu.make_async_copy(w_uv, uv_v, load_sem.at[2]),
        pltpu.make_async_copy(w_out, out_v, load_sem.at[3]),
        pltpu.make_async_copy(w_gate_up, gu_v, load_sem.at[4]),
        pltpu.make_async_copy(w_down.at[:, half], down_v.at[core], load_sem.at[5]),
    ]
    small = [
        pltpu.make_async_copy(src, dst, load_sem.at[6 + n])
        for n, (src, dst) in enumerate([
            (query_h, query), (new_latent_h, new_latent), (cache_len_h, cache_len), (hidden_in_h, hidden_in),
            (gain_h, gain), (routing_h, routing), (route_weight_h, route_weight),
        ])
    ]
    for copy in small[:3] + loads[:3] + small[3:] + loads[3:]:
        copy.start()
    for copy in small[:3]:
        copy.wait()

    scale = float(VH + ROPE) ** (-0.5)
    q_all = query[...].reshape(4 * XY, LAT)
    fresh = new_latent[...]
    near = mm(q_all, fresh, ((1,), (1,))) * scale
    row = lax.broadcasted_iota(jnp.int32, (64, 4), 0)
    col = lax.broadcasted_iota(jnp.int32, (64, 4), 1)
    near = jnp.where((row // 32 == col // 2) & (row // 16 >= col), near, -jnp.inf)
    contexts = []
    for b in range(2):
        loads[b].wait()
        q = q_all[32 * b : 32 * b + 32]
        far = mm(q, cache_v[b]) * scale
        place = lax.broadcasted_iota(jnp.int32, (32, MAXLEN), 1)
        far = jnp.where(place < cache_len[b], far, -jnp.inf)
        close = near[32 * b : 32 * b + 32]
        highest = jnp.maximum(
            jnp.max(far, axis=1, keepdims=True), jnp.max(close, axis=1, keepdims=True)
        )
        far = jnp.exp(far - highest)
        close = jnp.exp(close - highest)
        total = jnp.sum(far, axis=1, keepdims=True) + jnp.sum(close, axis=1, keepdims=True)
        context = mm((far / total).astype(BF16), cache_v[b, :KVL, :], ((1,), (1,)))
        context = context + mm((close / total).astype(BF16), fresh[:, :KVL])
        contexts.append(context.astype(BF16))
    context = jnp.concatenate(contexts, axis=0)
    loads[2].wait()
    row = lax.broadcasted_iota(jnp.int32, (64, VH), 0)
    head_out = jnp.zeros((64, VH), F32)
    for h in range(16):
        head_out = jnp.where(row % 16 == h, mm(context, uv_v[h]), head_out)
    heads_a[0] = head_out.astype(BF16)

    for copy in small[3:]:
        copy.wait()
    hidden[z, :, :COLS] = hidden_in[...]
    hidden[z, :, COLS:] = jnp.zeros((QTOK, WIDE - COLS), BF16)
    pl.semaphore_wait(barrier, XY + 3)

    def a_copy(k):
        return remote(heads_a.at[0], heads_a.at[k], a_s, a_r.at[(k - 1) // 5], peer(k) * 2 + core, z)

    def a2_copy(ks, sem):
        return remote(heads_a.at[ks], heads_b.at[ks], a2_s, sem, sib, z)

    for k in range(1, XY):
        a_copy(k).start()
    a2_copy(pl.ds(0, 1), a2_r.at[3]).start()

    def hid_copy(j):
        return remote(hidden.at[z], hidden.at[z], hid_s, hid_r, dp, zpeer(j))

    for j in range(1, 4):
        hid_copy(j).start()
    w_copy = remote(w_down.at[:, other_half], down_v.at[core], w_s, w_r, sib, z)
    w_copy.start()

    expert = lax.broadcasted_iota(jnp.int32, (EXPERTS, TOKENS), 0)
    member = jnp.zeros((EXPERTS, TOKENS), F32)
    share = jnp.zeros((1, TOKENS), F32)
    turn = (3 - z) * QTOK
    turned = pltpu.roll(routing[...], turn, 1)
    turned_weight = pltpu.roll(route_weight[...], turn, 1)
    for k in range(TOP):
        named = turned[k : k + 1, :]
        member = member + jnp.where(named == expert, 1.0, 0.0)
        share = share + jnp.where(named == xy, turned_weight[k : k + 1, :], 0.0)
    i0 = lax.broadcasted_iota(jnp.int32, (TOKENS, TOKENS), 0)
    i1 = lax.broadcasted_iota(jnp.int32, (TOKENS, TOKENS), 1)
    earlier = jnp.where((i0 < i1) & (i0 // QTOK == i1 // QTOK), 1.0, 0.0).astype(BF16)
    position = mm(member.astype(BF16), earlier)
    mem_t[...] = member
    pos_t[...] = position
    slot = lax.broadcasted_iota(jnp.int32, (ROWS, TOKENS), 0)
    token = lax.broadcasted_iota(jnp.int32, (ROWS, TOKENS), 1)
    in_block = slot // CAP == token // QTOK
    rank = (slot % CAP).astype(F32)
    for k in range(XY):
        e = pl.ds(peer(k), 1)
        here = (mem_t[e, :] > 0.5) & in_block & (pos_t[e, :] == rank)
        chosen = jnp.where(here, 1.0, 0.0)
        for h in range(2):
            pick[h, k] = chosen[h * PART : (h + 1) * PART, h * 2 * QTOK : (h + 1) * 2 * QTOK].astype(BF16)
        if k == 0:
            wcol[...] = jnp.broadcast_to(jnp.sum(chosen * share, axis=1, keepdims=True), (ROWS, 128))
    i0 = lax.broadcasted_iota(jnp.int32, (TOKENS, QTOK), 0)
    i1 = lax.broadcasted_iota(jnp.int32, (TOKENS, QTOK), 1)
    own = jnp.where(i0 == i1 + 3 * QTOK, 1.0, 0.0).astype(BF16)
    spread_e = lax.broadcasted_iota(jnp.int32, (EXPERTS, EXPERTS * 2 * CAP), 0)
    spread_c = lax.broadcasted_iota(jnp.int32, (EXPERTS, EXPERTS * 2 * CAP), 1)
    spread = jnp.where(spread_c // (2 * CAP) == spread_e, 1.0, 0.0).astype(BF16)
    mem_own = mm(mm(member.astype(BF16), own).astype(BF16), spread, ((0,), (0,)))
    pos_own = mm(mm(position.astype(BF16), own).astype(BF16), spread, ((0,), (0,)))
    place = lax.broadcasted_iota(jnp.int32, (QTOK, EXPERTS * 2 * CAP), 1)
    found = (mem_own > 0.5) & (pos_own == (place % CAP).astype(F32))
    first = place % (2 * CAP) < CAP
    merge[:QTOK, :] = jnp.where(found & first, 1.0, 0.0).astype(BF16)
    merge[QTOK:, :] = jnp.where(found & (place % (2 * CAP) >= CAP), 1.0, 0.0).astype(BF16)

    def spread_down(which):
        for m in range(16):
            first, last = COLS * m // 128, (COLS * (m + 1) + 127) // 128
            at = COLS * m - 128 * first
            piece = down_v[which, :, 128 * first : 128 * last][:, at : at + COLS]
            down_p[which, m, :, :COLS] = piece
            down_p[which, m, :, COLS:] = jnp.zeros((UNITS, WIDE - COLS), BF16)

    loads[5].wait()
    spread_down(core)
    def groups(buffer, sem):
        return remote(buffer, buffer, a_s, sem, sib, z)

    fives = [pl.ds(5 * g + 1, 5) for g in range(3)]

    def spread_heads(buffer, owner, ks):
        for k in ks:
            at = pl.multiple_of((source(k) * 2 + owner) * 64, 64)
            heads32[pl.ds(at, 64), :] = buffer[k].astype(F32)

    spread_heads(heads_a, core, [0])
    for g in range(3):
        groups(heads_a.at[fives[g]], a_r.at[g]).wait_recv()
        a2_copy(fives[g], a2_r.at[g]).start()
        spread_heads(heads_a, core, range(5 * g + 1, 5 * g + 6))
    a2_copy(pl.ds(0, 1), a2_r.at[3]).wait_recv()
    spread_heads(heads_b, 1 - core, [0])
    for g in range(3):
        a2_copy(fives[g], a2_r.at[g]).wait_recv()
        spread_heads(heads_b, 1 - core, range(5 * g + 1, 5 * g + 6))
    loads[3].wait()
    projected = jnp.zeros((TOKENS, COLS), F32)
    for h in range(0, 16, 2):
        lhs = jnp.concatenate(
            [heads32[pl.ds(h, TOKENS, stride=16), :], heads32[pl.ds(h + 1, TOKENS, stride=16), :]], axis=1
        ).astype(BF16)
        projected = projected + mm(lhs, out_v[:, VH * h : VH * (h + 2)], ((1,), (1,)))
    for q in range(5):
        block = projected[QTOK * (q % 4) : QTOK * (q % 4 + 1)]
        part[q, :, :COLS] = block.astype(BF16)
        part[q, :, COLS:] = jnp.zeros((QTOK, WIDE - COLS), BF16)
        if q < 4:
            proj[q] = block

    def c_copy(h, j):
        blocks = part.at[pl.ds((z + j + 1 + 2 * h) % 4, 2)]
        return remote(blocks, part_in.at[h, j], c_s, c_r.at[h * 4 + j], dp, zpeer(j))

    for h in range(2):
        for j in (2, 1, 3):
            c_copy(h, j).start()
    w_copy.wait_recv()
    spread_down(1 - core)
    remote(hidden.at[pl.ds(0, 3)], hidden.at[pl.ds(0, 3)], hid_s, hid_r, dp, zpeer(1)).wait_recv()
    lane = lax.broadcasted_iota(jnp.int32, (2 * QTOK, WIDE - COLS), 1)

    def rows_of(h):
        blocks = [(z + 1 + 2 * h) % 4, (z + 2 + 2 * h) % 4]
        mid = jnp.concatenate([proj[q] + hidden[q][:, :COLS].astype(F32) for q in blocks], axis=0)
        for j in (1, 3, 2):
            c_copy(h, j).wait_recv()
            mid = mid + part_in[h, j].reshape(2 * QTOK, WIDE)[:, :COLS].astype(F32)
        if h == 1:
            mid_s[...] = mid[QTOK:]
        square = jnp.sum(mid * mid, axis=1, keepdims=True)
        square_hi = square.astype(BF16).astype(F32)
        square_lo = square - square_hi
        spare = jnp.where(lane == 0, square_hi, jnp.where(lane == 1, square_lo, 0.0))
        return jnp.concatenate([(mid * gain[...]), spare], axis=1).astype(BF16)

    def e_copy(h, k):
        return remote(
            x_out.at[h, k], x_a.at[h, k], e_s, e_r.at[h * 3 + (k - 1) // 5], peer(k) * 2 + core, z
        )

    def e2_copy(h, ks, n):
        return remote(x_a.at[h, ks], x_b.at[h, ks], e2_s, e2_r.at[h * 4 + n], sib, z)

    for h in range(2):
        all_rows = rows_of(h)
        for first in range(1, XY, 5):
            rows = mm(pick[h, first : first + 5].reshape(5 * PART, 2 * QTOK), all_rows).astype(BF16)
            for k in range(first, first + 5):
                x_out[h, k] = rows[PART * (k - first) : PART * (k - first + 1)]
                e_copy(h, k).start()
        x_a[h, 0] = mm(pick[h, 0], all_rows).astype(BF16)
        e2_copy(h, pl.ds(0, 1), 3).start()
    loads[4].wait()

    def take(sums, buffer, h, ks, owner):
        gate, up, squares = sums
        for k in ks:
            x = buffer[h, k]
            at = pl.ds(pl.multiple_of((source(k) * 2 + owner) * COLS, 32), COLS)
            gate = gate + mm(x[:, :COLS], gu_v[0, at, :])
            up = up + mm(x[:, :COLS], gu_v[1, at, :])
            squares = squares + x[:, 128:].astype(F32)
        return gate, up, squares

    def arrive(h, g):
        groups(x_a.at[h, fives[g]], e_r.at[h * 3 + g]).wait_recv()
        e2_copy(h, fives[g], g).start()

    def take_a(sums, h, g):
        return take(sums, x_a, h, range(5 * g + 1, 5 * g + 6), core)

    def take_b(sums, h, g):
        e2_copy(h, fives[g], g).wait_recv()
        return take(sums, x_b, h, range(5 * g + 1, 5 * g + 6), 1 - core)

    def take_own(h):
        sums = (jnp.zeros((PART, UNITS), F32), jnp.zeros((PART, UNITS), F32), jnp.zeros((PART, 128), F32))
        sums = take(sums, x_a, h, [0], core)
        e2_copy(h, pl.ds(0, 1), 3).wait_recv()
        return take(sums, x_b, h, [0], 1 - core)

    def f_copy(h):
        return remote(act_s.at[core, h], act_s.at[core, h], f_s.at[h], f_r.at[h], sib, z)

    def activate(sums, h):
        gate, up, squares = sums
        square = squares[:, COLS - 128 : COLS - 127] + squares[:, COLS - 127 : COLS - 126]
        factor = lax.rsqrt(square / D + EPSILON)
        g = gate * factor
        u = up * factor
        act_s[core, h] = (g / (1.0 + jnp.exp(-g)) * u).astype(BF16)
        f_copy(h).start()

    def g_copy(m, q):
        return remote(y_out.at[m, q], y_in.at[z * XY + xy], g_s, g_r, core * 16 + m, (z + 1 + q) % 4)

    def g_self(m, q):
        return pltpu.make_async_copy(y_out.at[m, q], y_in.at[z * XY + xy], g_own)

    def results(h, n):
        group = (dp // 4 % 4 + n) % 4
        weight = wcol[PART * h : PART * (h + 1), :1]
        for k in range(4):
            m = group * 4 + k
            y = (mm(act_s[0, h], down_p[0, m]) + mm(act_s[1, h], down_p[1, m])) * weight
            low, high = y[:, :128], y[:, 128:]
            for q in range(2):
                at_q = slice(CAP * q, CAP * (q + 1))
                slab = jnp.concatenate([low[at_q], high[at_q]], axis=0)
                y_out[m, 2 * h + q] = slab.astype(BF16)
        for q in ((1, 0) if h == 0 else (2, 3)):
            for i in range(4):
                m = group * 4 + (dp + i) % 4
                if n == 0 and i == 0 and q == 3:
                    to_self = core * 16 + m == dp

                    @pl.when(to_self)
                    def _():
                        g_self(m, q).start()

                    @pl.when(jnp.logical_not(to_self))
                    def _():
                        g_copy(m, q).start()

                else:
                    g_copy(m, q).start()

    sums = take_own(0)
    for g in range(3):
        arrive(0, g)
        sums = take_a(sums, 0, g)
    for g in range(3):
        sums = take_b(sums, 0, g)
    activate(sums, 0)
    sums = take_own(1)
    f_copy(0).wait_recv()
    results(0, 3)
    arrive(1, 0)
    results(0, 2)
    arrive(1, 1)
    results(0, 1)
    arrive(1, 2)
    results(0, 0)
    sums = take_a(sums, 1, 0)
    sums = take_b(sums, 1, 0)
    sums = take_a(sums, 1, 1)
    sums = take_b(sums, 1, 1)
    sums = take_a(sums, 1, 2)
    sums = take_b(sums, 1, 2)
    activate(sums, 1)
    f_copy(1).wait_recv()
    for n in (3, 2, 1, 0):
        results(1, n)
    mine = side == core

    def slabs(count):
        return remote(y_in.at[pl.ds(0, count)], y_in.at[pl.ds(0, count)], g_s, g_r, sib, z)

    @pl.when(mine)
    def _():
        slabs(63).wait_recv()
        g_self(0, 0).wait()

    @pl.when(jnp.logical_not(mine))
    def _():
        slabs(64).wait_recv()

    total = jnp.zeros((2 * QTOK, 128), F32)
    for j in range(4):
        total = total + mm(merge[...], y_in[XY * j : XY * (j + 1)].reshape(XY * 2 * CAP, 128))
    total = jnp.concatenate([total[:QTOK], total[QTOK:, : COLS - 128]], axis=1)
    out[...] = (mid_s[...] + total).astype(BF16)

    def left(ref, sem):
        remote(ref, ref, sem, w_r, sib, z).wait_send()

    left(heads_a.at[pl.ds(0, 15)], a_s)
    left(heads_a, a2_s)
    left(hidden.at[pl.ds(0, 3)], hid_s)
    w_copy.wait_send()
    left(part_in.at[0, pl.ds(0, 3)], c_s)
    left(part_in.at[0, pl.ds(0, 3)], c_s)
    left(x_out.at[0], e_s)
    left(x_out.at[0, pl.ds(0, 14)], e_s)
    left(x_a, e2_s)
    for h in range(2):
        f_copy(h).wait_send()

    @pl.when(mine)
    def _():
        slabs(63).wait_send()

    @pl.when(jnp.logical_not(mine))
    def _():
        slabs(64).wait_send()


def on_device(
    query, new_latent, cache, cache_len, w_uv, w_out, hidden_in, norm_gain, routing, route_weight,
    w_gate_up, w_down,
):
    vmem = pl.BlockSpec(memory_space=pltpu.VMEM)
    hbm = pl.BlockSpec(memory_space=pl.ANY)
    dma = pltpu.SemaphoreType.DMA
    return pl.pallas_call(
        kernel,
        out_shape=jax.ShapeDtypeStruct((QTOK, COLS), BF16),
        in_specs=[hbm] * 12,
        out_specs=vmem,
        scratch_shapes=[
            pltpu.VMEM((4, 16, LAT), BF16),
            pltpu.VMEM((4, LAT), BF16),
            pltpu.SMEM((2,), jnp.int32),
            pltpu.VMEM((QTOK, COLS), BF16),
            pltpu.VMEM((1, COLS), F32),
            pltpu.VMEM((TOP, TOKENS), jnp.int32),
            pltpu.VMEM((TOP, TOKENS), F32),
            pltpu.VMEM((2, LAT, MAXLEN), BF16),
            pltpu.VMEM((16, KVL, VH), BF16),
            pltpu.VMEM((COLS, 16 * VH), BF16),
            pltpu.VMEM((2, D, UNITS), BF16),
            pltpu.VMEM((2, UNITS, HALF), BF16),
            pltpu.VMEM((2, XY, UNITS, WIDE), BF16),
            pltpu.VMEM((XY, 64, VH), BF16),
            pltpu.VMEM((XY, 64, VH), BF16),
            pltpu.VMEM((32 * 64, VH), F32),
            pltpu.VMEM((4, QTOK, COLS), F32),
            pltpu.VMEM((5, QTOK, WIDE), BF16),
            pltpu.VMEM((2, 4, 2, QTOK, WIDE), BF16),
            pltpu.VMEM((4, QTOK, WIDE), BF16),
            pltpu.VMEM((2, XY, PART, 2 * QTOK), BF16),
            pltpu.VMEM((EXPERTS, TOKENS), F32),
            pltpu.VMEM((EXPERTS, TOKENS), F32),
            pltpu.VMEM((QTOK, COLS), F32),
            pltpu.VMEM((ROWS, 128), F32),
            pltpu.VMEM((2 * QTOK, XY * 2 * CAP), BF16),
            pltpu.VMEM((2, XY, PART, WIDE), BF16),
            pltpu.VMEM((2, XY, PART, WIDE), BF16),
            pltpu.VMEM((2, XY, PART, WIDE), BF16),
            pltpu.VMEM((2, 2, PART, UNITS), BF16),
            pltpu.VMEM((XY, 4, 2 * CAP, 128), BF16),
            pltpu.VMEM((4 * XY, 2 * CAP, 128), BF16),
            dma((13,)),
            dma, dma, dma, dma,
            dma, dma((3,)), dma, dma((4,)),
            dma, dma((8,)),
            dma, dma((6,)), dma, dma((8,)),
            dma((2,)), dma((2,)), dma, dma, dma,
        ],
        compiler_params=pltpu.CompilerParams(
            collective_id=0, has_side_effects=True, vmem_limit_bytes=56 * 2**20
        ),
    )(
        query, new_latent, cache.transpose(0, 2, 1), cache_len, w_uv, w_out.T, hidden_in,
        norm_gain.reshape(1, COLS), routing.T, route_weight.T, w_gate_up, w_down,
    )


def solution(mesh):
    placed = (
        P("dp", "tp", None),
        P("dp", None),
        P("dp", None, None),
        P("dp"),
        P("tp", None, None),
        P("tp", "dp"),
        P("tp", "dp"),
        P("dp"),
        P(),
        P(),
        P(None, None, ("dp", "tp")),
        P(("dp", "tp"), None),
    )
    return jax.shard_map(
        on_device, mesh=mesh, in_specs=placed, out_specs=P("tp", "dp"), check_vma=False
    )
```

```python
import jax
import jax.numpy as jnp
from jax import lax
from jax.experimental import pallas as pl
from jax.experimental.pallas import tpu as pltpu
from jax.sharding import PartitionSpec as P

D = 7168
LAT = 576
KVL = 512
ROPE = 64
VH = 128
MAXLEN = 1024
EXPERTS = 16
TOKENS = 128
TOP = 8
QTOK = 32
CAP = 24
ROWS = 4 * CAP
COLS = 224
WIDE = 256
UNITS = 256
XY = 16
HALF = D // 2
PART = ROWS // 2
EPSILON = 1e-06
MESH = pl.DeviceIdType.MESH
F32 = jnp.float32
BF16 = jnp.bfloat16


def mm(a, b, dims=((1,), (0,)), precision=None):
    return lax.dot_general(a, b, (dims, ((), ())), preferred_element_type=F32, precision=precision)


OFFSETS = [(0, 0)] + sorted(
    [(a, b) for a in range(4) for b in range(4) if (a, b) != (0, 0)],
    key=lambda o: -(min(o[0], 4 - o[0]) + min(o[1], 4 - o[1])),
)


def kernel(
    query_h, new_latent_h, cache, cache_len_h, w_uv, w_out, hidden_in_h, gain_h, routing_h,
    route_weight_h, w_gate_up, w_down, out,
    query, new_latent, cache_len, hidden_in, gain, routing, route_weight, cache_v, uv_v, out_v, gu_v, down_v, down_p,
    heads_a, heads_b, heads32, proj, part, part_in, hidden, pick, mem_t, pos_t, mid_s, wcol, merge,
    x_out, x_a, x_b, act_s, y_out, y_in,
    load_sem, hid_s, hid_r, w_s, w_r, a_s, a_r, a2_s, a2_r, c_s, c_r, e_s, e_r, e2_s, e2_r,
    f_s, f_r, g_s, g_r, g_own,
):
    dp = lax.axis_index("dp")
    z = lax.axis_index("tp")
    xy = dp // 2
    core = dp % 2
    sib = xy * 2 + (1 - core)
    side = dp // 16

    def peer(k):
        return (xy // 4 + OFFSETS[k][0]) % 4 * 4 + (xy + OFFSETS[k][1]) % 4

    def source(k):
        return (xy // 4 + 4 - OFFSETS[k][0]) % 4 * 4 + (xy + 4 - OFFSETS[k][1]) % 4

    def zpeer(j):
        return (z + j) % 4

    def remote(src, dst, send, recv, to_dp, to_z):
        return pltpu.make_async_remote_copy(
            src_ref=src, dst_ref=dst, send_sem=send, recv_sem=recv,
            device_id=(to_dp, to_z), device_id_type=MESH,
        )

    def left(ref, sem):
        remote(ref, ref, sem, w_r, sib, z).wait_send()

    barrier = pltpu.get_barrier_semaphore()
    for k in range(1, XY):
        pl.semaphore_signal(barrier, inc=1, device_id=(peer(k) * 2 + core, z), device_id_type=MESH)
    for j in (2, 1, 3):
        pl.semaphore_signal(barrier, inc=1, device_id=(dp, zpeer(j)), device_id_type=MESH)
    pl.semaphore_signal(barrier, inc=1, device_id=(sib, z), device_id_type=MESH)

    half = pl.ds(pl.multiple_of(core * HALF, 128), HALF)
    other_half = pl.ds(pl.multiple_of((1 - core) * HALF, 128), HALF)
    loads = [
        pltpu.make_async_copy(cache.at[0], cache_v.at[0], load_sem.at[0]),
        pltpu.make_async_copy(cache.at[1], cache_v.at[1], load_sem.at[1]),
        pltpu.make_async_copy(w_uv, uv_v, load_sem.at[2]),
        pltpu.make_async_copy(w_out, out_v, load_sem.at[3]),
        pltpu.make_async_copy(w_gate_up, gu_v, load_sem.at[4]),
        pltpu.make_async_copy(w_down.at[:, half], down_v.at[core], load_sem.at[5]),
    ]
    small = [
        pltpu.make_async_copy(src, dst, load_sem.at[6 + n])
        for n, (src, dst) in enumerate([
            (query_h, query), (new_latent_h, new_latent), (cache_len_h, cache_len), (hidden_in_h, hidden_in),
            (gain_h, gain), (routing_h, routing), (route_weight_h, route_weight),
        ])
    ]
    for copy in small[:3] + loads[:3] + small[3:] + loads[3:]:
        copy.start()
    for copy in small[:3]:
        copy.wait()

    scale = float(VH + ROPE) ** (-0.5)
    q_all = query[...].reshape(4 * XY, LAT)
    fresh = new_latent[...]
    near = mm(q_all, fresh, ((1,), (1,))) * scale
    row = lax.broadcasted_iota(jnp.int32, (64, 4), 0)
    col = lax.broadcasted_iota(jnp.int32, (64, 4), 1)
    near = jnp.where((row // 32 == col // 2) & (row // 16 >= col), near, -jnp.inf)
    contexts = []
    for b in range(2):
        loads[b].wait()
        q = q_all[32 * b : 32 * b + 32]
        far = mm(q, cache_v[b]) * scale
        place = lax.broadcasted_iota(jnp.int32, (32, MAXLEN), 1)
        far = jnp.where(place < cache_len[b], far, -jnp.inf)
        close = near[32 * b : 32 * b + 32]
        highest = jnp.maximum(
            jnp.max(far, axis=1, keepdims=True), jnp.max(close, axis=1, keepdims=True)
        )
        far = jnp.exp(far - highest)
        close = jnp.exp(close - highest)
        total = jnp.sum(far, axis=1, keepdims=True) + jnp.sum(close, axis=1, keepdims=True)
        context = mm((far / total).astype(BF16), cache_v[b, :KVL, :], ((1,), (1,)))
        context = context + mm((close / total).astype(BF16), fresh[:, :KVL])
        contexts.append(context.astype(BF16))
    context = jnp.concatenate(contexts, axis=0)
    loads[2].wait()
    row = lax.broadcasted_iota(jnp.int32, (64, VH), 0)
    head_out = jnp.zeros((64, VH), F32)
    for h in range(16):
        head_out = jnp.where(row % 16 == h, mm(context, uv_v[h]), head_out)
    heads_a[0] = head_out.astype(BF16)

    for copy in small[3:]:
        copy.wait()
    hidden[z, :, :COLS] = hidden_in[...]
    hidden[z, :, COLS:] = jnp.zeros((QTOK, WIDE - COLS), BF16)
    pl.semaphore_wait(barrier, XY + 3)

    def a_copy(k):
        return remote(heads_a.at[0], heads_a.at[k], a_s, a_r.at[(k - 1) // 5], peer(k) * 2 + core, z)

    def a2_copy(ks, sem):
        return remote(heads_a.at[ks], heads_b.at[ks], a2_s, sem, sib, z)

    for k in range(1, XY):
        a_copy(k).start()
    a2_copy(pl.ds(0, 1), a2_r.at[3]).start()

    def hid_copy(j):
        return remote(hidden.at[z], hidden.at[z], hid_s, hid_r, dp, zpeer(j))

    for j in range(1, 4):
        hid_copy(j).start()
    w_copy = remote(w_down.at[:, other_half], down_v.at[core], w_s, w_r, sib, z)
    w_copy.start()

    expert = lax.broadcasted_iota(jnp.int32, (EXPERTS, TOKENS), 0)
    member = jnp.zeros((EXPERTS, TOKENS), F32)
    share = jnp.zeros((1, TOKENS), F32)
    turn = (3 - z) * QTOK
    turned = pltpu.roll(routing[...], turn, 1)
    turned_weight = pltpu.roll(route_weight[...], turn, 1)
    for k in range(TOP):
        named = turned[k : k + 1, :]
        member = member + jnp.where(named == expert, 1.0, 0.0)
        share = share + jnp.where(named == xy, turned_weight[k : k + 1, :], 0.0)
    i0 = lax.broadcasted_iota(jnp.int32, (TOKENS, TOKENS), 0)
    i1 = lax.broadcasted_iota(jnp.int32, (TOKENS, TOKENS), 1)
    earlier = jnp.where((i0 < i1) & (i0 // QTOK == i1 // QTOK), 1.0, 0.0).astype(BF16)
    position = mm(member.astype(BF16), earlier)
    mem_t[...] = member
    pos_t[...] = position
    slot = lax.broadcasted_iota(jnp.int32, (ROWS, TOKENS), 0)
    token = lax.broadcasted_iota(jnp.int32, (ROWS, TOKENS), 1)
    in_block = slot // CAP == token // QTOK
    rank = (slot % CAP).astype(F32)
    for k in range(XY):
        e = pl.ds(peer(k), 1)
        here = (mem_t[e, :] > 0.5) & in_block & (pos_t[e, :] == rank)
        chosen = jnp.where(here, 1.0, 0.0)
        for h in range(2):
            pick[h, k] = chosen[h * PART : (h + 1) * PART, h * 2 * QTOK : (h + 1) * 2 * QTOK].astype(BF16)
        if k == 0:
            wcol[...] = jnp.broadcast_to(jnp.sum(chosen * share, axis=1, keepdims=True), (ROWS, 128))
    i0 = lax.broadcasted_iota(jnp.int32, (TOKENS, QTOK), 0)
    i1 = lax.broadcasted_iota(jnp.int32, (TOKENS, QTOK), 1)
    own = jnp.where(i0 == i1 + 3 * QTOK, 1.0, 0.0).astype(BF16)
    spread_e = lax.broadcasted_iota(jnp.int32, (EXPERTS, EXPERTS * 2 * CAP), 0)
    spread_c = lax.broadcasted_iota(jnp.int32, (EXPERTS, EXPERTS * 2 * CAP), 1)
    spread = jnp.where(spread_c // (2 * CAP) == spread_e, 1.0, 0.0).astype(BF16)
    mem_own = mm(mm(member.astype(BF16), own).astype(BF16), spread, ((0,), (0,)))
    pos_own = mm(mm(position.astype(BF16), own).astype(BF16), spread, ((0,), (0,)))
    place = lax.broadcasted_iota(jnp.int32, (QTOK, EXPERTS * 2 * CAP), 1)
    found = (mem_own > 0.5) & (pos_own == (place % CAP).astype(F32))
    first = place % (2 * CAP) < CAP
    merge[:QTOK, :] = jnp.where(found & first, 1.0, 0.0).astype(BF16)
    merge[QTOK:, :] = jnp.where(found & (place % (2 * CAP) >= CAP), 1.0, 0.0).astype(BF16)

    def spread_down(which):
        units = pl.ds(pl.multiple_of(which * UNITS, UNITS), UNITS)
        for m in range(16):
            first, last = COLS * m // 128, (COLS * (m + 1) + 127) // 128
            at = COLS * m - 128 * first
            piece = down_v[which, :, 128 * first : 128 * last][:, at : at + COLS]
            down_p[m, units, :COLS] = piece
            down_p[m, units, COLS:] = jnp.zeros((UNITS, WIDE - COLS), BF16)

    loads[5].wait()
    spread_down(core)
    def groups(buffer, sem):
        return remote(buffer, buffer, a_s, sem, sib, z)

    fives = [pl.ds(5 * g + 1, 5) for g in range(3)]

    def spread_heads(buffer, owner, ks):
        for k in ks:
            at = pl.multiple_of((source(k) * 2 + owner) * 64, 64)
            heads32[pl.ds(at, 64), :] = buffer[k].astype(F32)

    spread_heads(heads_a, core, [0])
    for g in range(3):
        groups(heads_a.at[fives[g]], a_r.at[g]).wait_recv()
        a2_copy(fives[g], a2_r.at[g]).start()
        spread_heads(heads_a, core, range(5 * g + 1, 5 * g + 6))
    a2_copy(pl.ds(0, 1), a2_r.at[3]).wait_recv()
    spread_heads(heads_b, 1 - core, [0])
    for g in range(3):
        a2_copy(fives[g], a2_r.at[g]).wait_recv()
        spread_heads(heads_b, 1 - core, range(5 * g + 1, 5 * g + 6))
    loads[3].wait()
    projected = jnp.zeros((TOKENS, COLS), F32)
    for h in range(0, 16, 2):
        lhs = jnp.concatenate(
            [heads32[pl.ds(h, TOKENS, stride=16), :], heads32[pl.ds(h + 1, TOKENS, stride=16), :]], axis=1
        ).astype(BF16)
        projected = projected + mm(lhs, out_v[:, VH * h : VH * (h + 2)], ((1,), (1,)))
    for q in range(5):
        block = projected[QTOK * (q % 4) : QTOK * (q % 4 + 1)]
        part[q, :, :COLS] = block.astype(BF16)
        part[q, :, COLS:] = jnp.zeros((QTOK, WIDE - COLS), BF16)
        if q < 4:
            proj[q] = block

    def c_copy(h, j):
        blocks = part.at[pl.ds((z + j + 1 + 2 * h) % 4, 2)]
        return remote(blocks, part_in.at[h, j], c_s.at[h], c_r.at[h * 4 + j], dp, zpeer(j))

    for h in range(2):
        for j in (2, 1, 3):
            c_copy(h, j).start()
        if h == 0:
            left(part_in.at[0, pl.ds(0, 3)], c_s.at[0])
    w_copy.wait_recv()
    spread_down(1 - core)
    remote(hidden.at[pl.ds(0, 3)], hidden.at[pl.ds(0, 3)], hid_s, hid_r, dp, zpeer(1)).wait_recv()
    lane = lax.broadcasted_iota(jnp.int32, (2 * QTOK, WIDE - COLS), 1)

    def rows_of(h):
        blocks = [(z + 1 + 2 * h) % 4, (z + 2 + 2 * h) % 4]
        mid = jnp.concatenate([proj[q] + hidden[q][:, :COLS].astype(F32) for q in blocks], axis=0)
        for j in (1, 3, 2):
            c_copy(h, j).wait_recv()
            mid = mid + part_in[h, j].reshape(2 * QTOK, WIDE)[:, :COLS].astype(F32)
        if h == 1:
            mid_s[...] = mid[QTOK:]
        square = jnp.sum(mid * mid, axis=1, keepdims=True)
        square_hi = square.astype(BF16).astype(F32)
        square_lo = square - square_hi
        spare = jnp.where(lane == 0, square_hi, jnp.where(lane == 1, square_lo, 0.0))
        return jnp.concatenate([(mid * gain[...]), spare], axis=1).astype(BF16)

    def e_copy(h, k):
        return remote(
            x_out.at[h, k], x_a.at[h, k], e_s.at[h], e_r.at[h * 3 + (k - 1) // 5], peer(k) * 2 + core, z
        )

    def e2_copy(h, ks, n):
        return remote(x_a.at[h, ks], x_b.at[h, ks], e2_s, e2_r.at[h * 4 + n], sib, z)

    for h in range(2):
        all_rows = rows_of(h)
        if h == 1:
            left(x_out.at[0, pl.ds(0, 15)], e_s.at[0])
        for first in range(1, XY, 5):
            rows = mm(pick[h, first : first + 5].reshape(5 * PART, 2 * QTOK), all_rows).astype(BF16)
            for k in range(first, first + 5):
                x_out[h, k] = rows[PART * (k - first) : PART * (k - first + 1)]
                e_copy(h, k).start()
        x_a[h, 0] = mm(pick[h, 0], all_rows).astype(BF16)
        e2_copy(h, pl.ds(0, 1), 3).start()
    loads[4].wait()

    def take(sums, buffer, h, ks, owner):
        gate, up, squares = sums
        for k in ks:
            x = buffer[h, k]
            at = pl.ds(pl.multiple_of((source(k) * 2 + owner) * COLS, 32), COLS)
            gate = gate + mm(x[:, :COLS], gu_v[0, at, :])
            up = up + mm(x[:, :COLS], gu_v[1, at, :])
            squares = squares + x[:, 128:].astype(F32)
        return gate, up, squares

    def arrive(h, g):
        groups(x_a.at[h, fives[g]], e_r.at[h * 3 + g]).wait_recv()
        e2_copy(h, fives[g], g).start()

    def take_a(sums, h, g):
        return take(sums, x_a, h, range(5 * g + 1, 5 * g + 6), core)

    def take_b(sums, h, g):
        e2_copy(h, fives[g], g).wait_recv()
        return take(sums, x_b, h, range(5 * g + 1, 5 * g + 6), 1 - core)

    def take_own(h):
        sums = (jnp.zeros((PART, UNITS), F32), jnp.zeros((PART, UNITS), F32), jnp.zeros((PART, 128), F32))
        sums = take(sums, x_a, h, [0], core)
        e2_copy(h, pl.ds(0, 1), 3).wait_recv()
        return take(sums, x_b, h, [0], 1 - core)

    def f_copy(h):
        return remote(act_s.at[core, h], act_s.at[core, h], f_s.at[h], f_r.at[h], sib, z)

    def activate(sums, h):
        gate, up, squares = sums
        square = squares[:, COLS - 128 : COLS - 127] + squares[:, COLS - 127 : COLS - 126]
        factor = lax.rsqrt(square / D + EPSILON)
        g = gate * factor
        u = up * factor
        act_s[core, h] = (g / (1.0 + jnp.exp(-g)) * u).astype(BF16)
        f_copy(h).start()

    def g_copy(m, q):
        return remote(y_out.at[m, q], y_in.at[z * XY + xy], g_s, g_r, core * 16 + m, (z + 1 + q) % 4)

    def g_self(m, q):
        return pltpu.make_async_copy(y_out.at[m, q], y_in.at[z * XY + xy], g_own)

    def results(h, n):
        group = (dp // 4 % 4 + n) % 4
        weight = wcol[PART * h : PART * (h + 1), :1]
        act = jnp.concatenate([act_s[0, h], act_s[1, h]], axis=1)
        for k in range(4):
            m = group * 4 + k
            y = mm(act, down_p[m]) * weight
            low, high = y[:, :128], y[:, 128:]
            for q in range(2):
                at_q = slice(CAP * q, CAP * (q + 1))
                slab = jnp.concatenate([low[at_q], high[at_q]], axis=0)
                y_out[m, 2 * h + q] = slab.astype(BF16)
        for q in ((1, 0) if h == 0 else (2, 3)):
            for i in range(4):
                m = group * 4 + (dp + i) % 4
                if n == 0 and i == 0 and q == 3:
                    to_self = core * 16 + m == dp

                    @pl.when(to_self)
                    def _():
                        g_self(m, q).start()

                    @pl.when(jnp.logical_not(to_self))
                    def _():
                        g_copy(m, q).start()

                else:
                    g_copy(m, q).start()

    sums = take_own(0)
    for g in range(3):
        arrive(0, g)
        sums = take_a(sums, 0, g)
    for g in range(3):
        sums = take_b(sums, 0, g)
    activate(sums, 0)
    sums = take_own(1)
    f_copy(0).wait_recv()
    results(0, 3)
    arrive(1, 0)
    results(0, 2)
    arrive(1, 1)
    results(0, 1)
    arrive(1, 2)
    results(0, 0)
    sums = take_a(sums, 1, 0)
    sums = take_b(sums, 1, 0)
    sums = take_a(sums, 1, 1)
    sums = take_b(sums, 1, 1)
    sums = take_a(sums, 1, 2)
    sums = take_b(sums, 1, 2)
    activate(sums, 1)
    f_copy(1).wait_recv()
    for n in (3, 2, 1, 0):
        results(1, n)
    mine = side == core

    def slabs(count):
        return remote(y_in.at[pl.ds(0, count)], y_in.at[pl.ds(0, count)], g_s, g_r, sib, z)


    left(heads_a.at[pl.ds(0, 15)], a_s)
    left(heads_a, a2_s)
    left(hidden.at[pl.ds(0, 3)], hid_s)
    w_copy.wait_send()
    left(part_in.at[1, pl.ds(0, 3)], c_s.at[1])
    left(x_out.at[1, pl.ds(0, 15)], e_s.at[1])
    left(x_a, e2_s)
    for h in range(2):
        f_copy(h).wait_send()

    @pl.when(mine)
    def _():
        slabs(63).wait_recv()
        g_self(0, 0).wait()

    @pl.when(jnp.logical_not(mine))
    def _():
        slabs(64).wait_recv()

    total = jnp.zeros((2 * QTOK, 128), F32)
    for j in range(4):
        total = total + mm(merge[...], y_in[XY * j : XY * (j + 1)].reshape(XY * 2 * CAP, 128))
    total = jnp.concatenate([total[:QTOK], total[QTOK:, : COLS - 128]], axis=1)
    out[...] = (mid_s[...] + total).astype(BF16)

    @pl.when(mine)
    def _():
        slabs(63).wait_send()

    @pl.when(jnp.logical_not(mine))
    def _():
        slabs(64).wait_send()


def on_device(
    query, new_latent, cache, cache_len, w_uv, w_out, hidden_in, norm_gain, routing, route_weight,
    w_gate_up, w_down,
):
    vmem = pl.BlockSpec(memory_space=pltpu.VMEM)
    hbm = pl.BlockSpec(memory_space=pl.ANY)
    dma = pltpu.SemaphoreType.DMA
    return pl.pallas_call(
        kernel,
        out_shape=jax.ShapeDtypeStruct((QTOK, COLS), BF16),
        in_specs=[hbm] * 12,
        out_specs=vmem,
        scratch_shapes=[
            pltpu.VMEM((4, 16, LAT), BF16),
            pltpu.VMEM((4, LAT), BF16),
            pltpu.SMEM((2,), jnp.int32),
            pltpu.VMEM((QTOK, COLS), BF16),
            pltpu.VMEM((1, COLS), F32),
            pltpu.VMEM((TOP, TOKENS), jnp.int32),
            pltpu.VMEM((TOP, TOKENS), F32),
            pltpu.VMEM((2, LAT, MAXLEN), BF16),
            pltpu.VMEM((16, KVL, VH), BF16),
            pltpu.VMEM((COLS, 16 * VH), BF16),
            pltpu.VMEM((2, D, UNITS), BF16),
            pltpu.VMEM((2, UNITS, HALF), BF16),
            pltpu.VMEM((XY, 2 * UNITS, WIDE), BF16),
            pltpu.VMEM((XY, 64, VH), BF16),
            pltpu.VMEM((XY, 64, VH), BF16),
            pltpu.VMEM((32 * 64, VH), F32),
            pltpu.VMEM((4, QTOK, COLS), F32),
            pltpu.VMEM((5, QTOK, WIDE), BF16),
            pltpu.VMEM((2, 4, 2, QTOK, WIDE), BF16),
            pltpu.VMEM((4, QTOK, WIDE), BF16),
            pltpu.VMEM((2, XY, PART, 2 * QTOK), BF16),
            pltpu.VMEM((EXPERTS, TOKENS), F32),
            pltpu.VMEM((EXPERTS, TOKENS), F32),
            pltpu.VMEM((QTOK, COLS), F32),
            pltpu.VMEM((ROWS, 128), F32),
            pltpu.VMEM((2 * QTOK, XY * 2 * CAP), BF16),
            pltpu.VMEM((2, XY, PART, WIDE), BF16),
            pltpu.VMEM((2, XY, PART, WIDE), BF16),
            pltpu.VMEM((2, XY, PART, WIDE), BF16),
            pltpu.VMEM((2, 2, PART, UNITS), BF16),
            pltpu.VMEM((XY, 4, 2 * CAP, 128), BF16),
            pltpu.VMEM((4 * XY, 2 * CAP, 128), BF16),
            dma((13,)),
            dma, dma, dma, dma,
            dma, dma((3,)), dma, dma((4,)),
            dma((2,)), dma((8,)),
            dma((2,)), dma((6,)), dma, dma((8,)),
            dma((2,)), dma((2,)), dma, dma, dma,
        ],
        compiler_params=pltpu.CompilerParams(
            collective_id=0, has_side_effects=True, vmem_limit_bytes=56 * 2**20
        ),
    )(
        query, new_latent, cache.transpose(0, 2, 1), cache_len, w_uv, w_out.T, hidden_in,
        norm_gain.reshape(1, COLS), routing.T, route_weight.T, w_gate_up, w_down,
    )


def solution(mesh):
    placed = (
        P("dp", "tp", None),
        P("dp", None),
        P("dp", None, None),
        P("dp"),
        P("tp", None, None),
        P("tp", "dp"),
        P("tp", "dp"),
        P("dp"),
        P(),
        P(),
        P(None, None, ("dp", "tp")),
        P(("dp", "tp"), None),
    )
    return jax.shard_map(
        on_device, mesh=mesh, in_specs=placed, out_specs=P("tp", "dp"), check_vma=False
    )
```

```python
import jax
import jax.numpy as jnp
from jax import lax
from jax.experimental import pallas as pl
from jax.experimental.pallas import tpu as pltpu
from jax.sharding import PartitionSpec as P

D = 7168
LAT = 576
KVL = 512
ROPE = 64
VH = 128
MAXLEN = 1024
EXPERTS = 16
TOKENS = 128
TOP = 8
QTOK = 32
CAP = 24
ROWS = 4 * CAP
COLS = 224
WIDE = 256
UNITS = 256
XY = 16
HALF = D // 2
PART = ROWS // 2
EPSILON = 1e-06
MESH = pl.DeviceIdType.MESH
F32 = jnp.float32
BF16 = jnp.bfloat16


def mm(a, b, dims=((1,), (0,)), precision=None):
    return lax.dot_general(a, b, (dims, ((), ())), preferred_element_type=F32, precision=precision)


OFFSETS = [(0, 0)] + sorted(
    [(a, b) for a in range(4) for b in range(4) if (a, b) != (0, 0)],
    key=lambda o: -(min(o[0], 4 - o[0]) + min(o[1], 4 - o[1])),
)


def kernel(
    query_h, new_latent_h, cache, cache_len_h, w_uv, w_out, hidden_in_h, gain_h, routing_h,
    route_weight_h, w_gate_up, w_down, out,
    query, new_latent, cache_len, hidden_in, gain, routing, route_weight, cache_v, uv_v, out_v, gu_v, down_v, down_p,
    heads_a, heads_b, heads32, proj, part, part_in, hidden, pick, mem_t, pos_t, mid_s, wcol, merge,
    x_out, x_a, x_b, act_s, y_out, y_in,
    load_sem, hid_s, hid_r, w_s, w_r, a_s, a_r, a2_s, a2_r, c_s, c_r, e_s, e_r, e2_s, e2_r,
    f_s, f_r, g_s, g_r, g_own,
):
    dp = lax.axis_index("dp")
    z = lax.axis_index("tp")
    xy = dp // 2
    core = dp % 2
    sib = xy * 2 + (1 - core)
    side = dp // 16

    def peer(k):
        return (xy // 4 + OFFSETS[k][0]) % 4 * 4 + (xy + OFFSETS[k][1]) % 4

    def source(k):
        return (xy // 4 + 4 - OFFSETS[k][0]) % 4 * 4 + (xy + 4 - OFFSETS[k][1]) % 4

    def zpeer(j):
        return (z + j) % 4

    def remote(src, dst, send, recv, to_dp, to_z):
        return pltpu.make_async_remote_copy(
            src_ref=src, dst_ref=dst, send_sem=send, recv_sem=recv,
            device_id=(to_dp, to_z), device_id_type=MESH,
        )

    def left(ref, sem):
        remote(ref, ref, sem, w_r, sib, z).wait_send()

    barrier = pltpu.get_barrier_semaphore()
    for k in range(1, XY):
        pl.semaphore_signal(barrier, inc=1, device_id=(peer(k) * 2 + core, z), device_id_type=MESH)
    for j in (2, 1, 3):
        pl.semaphore_signal(barrier, inc=1, device_id=(dp, zpeer(j)), device_id_type=MESH)
    pl.semaphore_signal(barrier, inc=1, device_id=(sib, z), device_id_type=MESH)

    half = pl.ds(pl.multiple_of(core * HALF, 128), HALF)
    other_half = pl.ds(pl.multiple_of((1 - core) * HALF, 128), HALF)
    loads = [
        pltpu.make_async_copy(cache.at[0], cache_v.at[0], load_sem.at[0]),
        pltpu.make_async_copy(cache.at[1], cache_v.at[1], load_sem.at[1]),
        pltpu.make_async_copy(w_uv, uv_v, load_sem.at[2]),
        pltpu.make_async_copy(w_out, out_v, load_sem.at[3]),
        pltpu.make_async_copy(w_gate_up, gu_v, load_sem.at[4]),
        pltpu.make_async_copy(w_down.at[:, half], down_v.at[core], load_sem.at[5]),
    ]
    small = [
        pltpu.make_async_copy(src, dst, load_sem.at[6 + n])
        for n, (src, dst) in enumerate([
            (query_h, query), (new_latent_h, new_latent), (cache_len_h, cache_len), (hidden_in_h, hidden_in),
            (gain_h, gain), (routing_h, routing), (route_weight_h, route_weight),
        ])
    ]
    for copy in small[:3] + loads[:3] + small[3:] + loads[3:]:
        copy.start()
    for copy in small[:3]:
        copy.wait()

    scale = float(VH + ROPE) ** (-0.5)
    q_all = query[...].reshape(4 * XY, LAT)
    fresh = new_latent[...]
    near = mm(q_all, fresh, ((1,), (1,))) * scale
    row = lax.broadcasted_iota(jnp.int32, (64, 4), 0)
    col = lax.broadcasted_iota(jnp.int32, (64, 4), 1)
    near = jnp.where((row // 32 == col // 2) & (row // 16 >= col), near, -jnp.inf)
    contexts = []
    for b in range(2):
        loads[b].wait()
        q = q_all[32 * b : 32 * b + 32]
        far = mm(q, cache_v[b]) * scale
        place = lax.broadcasted_iota(jnp.int32, (32, MAXLEN), 1)
        far = jnp.where(place < cache_len[b], far, -jnp.inf)
        close = near[32 * b : 32 * b + 32]
        highest = jnp.maximum(
            jnp.max(far, axis=1, keepdims=True), jnp.max(close, axis=1, keepdims=True)
        )
        far = jnp.exp(far - highest)
        close = jnp.exp(close - highest)
        total = jnp.sum(far, axis=1, keepdims=True) + jnp.sum(close, axis=1, keepdims=True)
        context = mm((far / total).astype(BF16), cache_v[b, :KVL, :], ((1,), (1,)))
        context = context + mm((close / total).astype(BF16), fresh[:, :KVL])
        contexts.append(context.astype(BF16))
    context = jnp.concatenate(contexts, axis=0)
    loads[2].wait()
    row = lax.broadcasted_iota(jnp.int32, (64, VH), 0)
    head_out = jnp.zeros((64, VH), F32)
    for h in range(16):
        head_out = jnp.where(row % 16 == h, mm(context, uv_v[h]), head_out)
    heads_a[0] = head_out.astype(BF16)

    for copy in small[3:]:
        copy.wait()
    hidden[z, :, :COLS] = hidden_in[...]
    hidden[z, :, COLS:] = jnp.zeros((QTOK, WIDE - COLS), BF16)
    pl.semaphore_wait(barrier, XY + 3)

    def a_copy(k):
        return remote(heads_a.at[0], heads_a.at[k], a_s, a_r.at[(k - 1) // 5], peer(k) * 2 + core, z)

    def a2_copy(ks, sem):
        return remote(heads_a.at[ks], heads_b.at[ks], a2_s, sem, sib, z)

    for k in range(1, XY):
        a_copy(k).start()
    a2_copy(pl.ds(0, 1), a2_r.at[3]).start()

    def hid_copy(j):
        return remote(hidden.at[z], hidden.at[z], hid_s, hid_r, dp, zpeer(j))

    for j in range(1, 4):
        hid_copy(j).start()
    w_copy = remote(w_down.at[:, other_half], down_v.at[core], w_s, w_r, sib, z)
    w_copy.start()

    expert = lax.broadcasted_iota(jnp.int32, (EXPERTS, TOKENS), 0)
    member = jnp.zeros((EXPERTS, TOKENS), F32)
    share = jnp.zeros((1, TOKENS), F32)
    turn = (3 - z) * QTOK
    turned = pltpu.roll(routing[...], turn, 1)
    turned_weight = pltpu.roll(route_weight[...], turn, 1)
    for k in range(TOP):
        named = turned[k : k + 1, :]
        member = member + jnp.where(named == expert, 1.0, 0.0)
        share = share + jnp.where(named == xy, turned_weight[k : k + 1, :], 0.0)
    i0 = lax.broadcasted_iota(jnp.int32, (TOKENS, TOKENS), 0)
    i1 = lax.broadcasted_iota(jnp.int32, (TOKENS, TOKENS), 1)
    earlier = jnp.where((i0 < i1) & (i0 // QTOK == i1 // QTOK), 1.0, 0.0).astype(BF16)
    position = mm(member.astype(BF16), earlier)
    mem_t[...] = member
    pos_t[...] = position
    slot = lax.broadcasted_iota(jnp.int32, (ROWS, TOKENS), 0)
    token = lax.broadcasted_iota(jnp.int32, (ROWS, TOKENS), 1)
    in_block = slot // CAP == token // QTOK
    rank = (slot % CAP).astype(F32)
    for k in range(XY):
        e = pl.ds(peer(k), 1)
        here = (mem_t[e, :] > 0.5) & in_block & (pos_t[e, :] == rank)
        chosen = jnp.where(here, 1.0, 0.0)
        for h in range(2):
            pick[h, k] = chosen[h * PART : (h + 1) * PART, h * 2 * QTOK : (h + 1) * 2 * QTOK].astype(BF16)
        if k == 0:
            wcol[...] = jnp.broadcast_to(jnp.sum(chosen * share, axis=1, keepdims=True), (ROWS, 128))
    i0 = lax.broadcasted_iota(jnp.int32, (TOKENS, QTOK), 0)
    i1 = lax.broadcasted_iota(jnp.int32, (TOKENS, QTOK), 1)
    own = jnp.where(i0 == i1 + 3 * QTOK, 1.0, 0.0).astype(BF16)
    spread_e = lax.broadcasted_iota(jnp.int32, (EXPERTS, EXPERTS * 2 * CAP), 0)
    spread_c = lax.broadcasted_iota(jnp.int32, (EXPERTS, EXPERTS * 2 * CAP), 1)
    spread = jnp.where(spread_c // (2 * CAP) == spread_e, 1.0, 0.0).astype(BF16)
    mem_own = mm(mm(member.astype(BF16), own).astype(BF16), spread, ((0,), (0,)))
    pos_own = mm(mm(position.astype(BF16), own).astype(BF16), spread, ((0,), (0,)))
    place = lax.broadcasted_iota(jnp.int32, (QTOK, EXPERTS * 2 * CAP), 1)
    found = (mem_own > 0.5) & (pos_own == (place % CAP).astype(F32))
    first = place % (2 * CAP) < CAP
    merge[:QTOK, :] = jnp.where(found & first, 1.0, 0.0).astype(BF16)
    merge[QTOK:, :] = jnp.where(found & (place % (2 * CAP) >= CAP), 1.0, 0.0).astype(BF16)

    def spread_down(which):
        units = pl.ds(pl.multiple_of(which * UNITS, UNITS), UNITS)
        for m in range(16):
            first, last = COLS * m // 128, (COLS * (m + 1) + 127) // 128
            at = COLS * m - 128 * first
            piece = down_v[which, :, 128 * first : 128 * last][:, at : at + COLS]
            down_p[m, units, :COLS] = piece
            down_p[m, units, COLS:] = jnp.zeros((UNITS, WIDE - COLS), BF16)

    loads[5].wait()
    spread_down(core)
    def groups(buffer, sem):
        return remote(buffer, buffer, a_s, sem, sib, z)

    fives = [pl.ds(5 * g + 1, 5) for g in range(3)]

    def spread_heads(buffer, owner, ks):
        for k in ks:
            at = pl.multiple_of((source(k) * 2 + owner) * 64, 64)
            heads32[pl.ds(at, 64), :] = buffer[k].astype(F32)

    spread_heads(heads_a, core, [0])
    for g in range(3):
        groups(heads_a.at[fives[g]], a_r.at[g]).wait_recv()
        a2_copy(fives[g], a2_r.at[g]).start()
        spread_heads(heads_a, core, range(5 * g + 1, 5 * g + 6))
    a2_copy(pl.ds(0, 1), a2_r.at[3]).wait_recv()
    spread_heads(heads_b, 1 - core, [0])
    for g in range(3):
        a2_copy(fives[g], a2_r.at[g]).wait_recv()
        spread_heads(heads_b, 1 - core, range(5 * g + 1, 5 * g + 6))
    loads[3].wait()
    projected = jnp.zeros((TOKENS, COLS), F32)
    for h in range(0, 16, 2):
        lhs = jnp.concatenate(
            [heads32[pl.ds(h, TOKENS, stride=16), :], heads32[pl.ds(h + 1, TOKENS, stride=16), :]], axis=1
        ).astype(BF16)
        projected = projected + mm(lhs, out_v[:, VH * h : VH * (h + 2)], ((1,), (1,)))
    for q in range(5):
        block = projected[QTOK * (q % 4) : QTOK * (q % 4 + 1)]
        part[q, :, :COLS] = block.astype(BF16)
        part[q, :, COLS:] = jnp.zeros((QTOK, WIDE - COLS), BF16)
        if q < 4:
            proj[q] = block

    def c_copy(h, j):
        blocks = part.at[pl.ds((z + j + 1 + 2 * h) % 4, 2)]
        return remote(blocks, part_in.at[h, j], c_s.at[h], c_r.at[h * 4 + j], dp, zpeer(j))

    for h in range(2):
        for j in (2, 1, 3):
            c_copy(h, j).start()
        if h == 0:
            left(part_in.at[0, pl.ds(0, 3)], c_s.at[0])
    w_copy.wait_recv()
    spread_down(1 - core)
    remote(hidden.at[pl.ds(0, 3)], hidden.at[pl.ds(0, 3)], hid_s, hid_r, dp, zpeer(1)).wait_recv()
    lane = lax.broadcasted_iota(jnp.int32, (2 * QTOK, WIDE - COLS), 1)

    def rows_of(h):
        blocks = [(z + 1 + 2 * h) % 4, (z + 2 + 2 * h) % 4]
        mid = jnp.concatenate([proj[q] + hidden[q][:, :COLS].astype(F32) for q in blocks], axis=0)
        for j in (1, 3, 2):
            c_copy(h, j).wait_recv()
            mid = mid + part_in[h, j].reshape(2 * QTOK, WIDE)[:, :COLS].astype(F32)
        if h == 1:
            mid_s[...] = mid[QTOK:]
        square = jnp.sum(mid * mid, axis=1, keepdims=True)
        square_hi = square.astype(BF16).astype(F32)
        square_lo = square - square_hi
        spare = jnp.where(lane == 0, square_hi, jnp.where(lane == 1, square_lo, 0.0))
        return jnp.concatenate([(mid * gain[...]), spare], axis=1).astype(BF16)

    def e_copy(h, k):
        return remote(
            x_out.at[h, k], x_a.at[h, k], e_s.at[h * 3 + (k - 1) // 5], e_r.at[h * 3 + (k - 1) // 5], peer(k) * 2 + core, z
        )

    def e2_copy(h, ks, n):
        return remote(x_a.at[h, ks], x_b.at[h, ks], e2_s, e2_r.at[h * 4 + n], sib, z)

    for h in range(2):
        all_rows = rows_of(h)
        if h == 1:
            for n in range(2):
                left(x_out.at[0, pl.ds(0, 5)], e_s.at[n])
        for first in range(1, XY, 5):
            rows = mm(pick[h, first : first + 5].reshape(5 * PART, 2 * QTOK), all_rows).astype(BF16)
            for k in range(first, first + 5):
                x_out[h, k] = rows[PART * (k - first) : PART * (k - first + 1)]
                e_copy(h, k).start()
        x_a[h, 0] = mm(pick[h, 0], all_rows).astype(BF16)
        e2_copy(h, pl.ds(0, 1), 3).start()
    loads[4].wait()

    def take(sums, buffer, h, ks, owner):
        gate, up, squares = sums
        for k in ks:
            x = buffer[h, k]
            at = pl.ds(pl.multiple_of((source(k) * 2 + owner) * COLS, 32), COLS)
            gate = gate + mm(x[:, :COLS], gu_v[0, at, :])
            up = up + mm(x[:, :COLS], gu_v[1, at, :])
            squares = squares + x[:, 128:].astype(F32)
        return gate, up, squares

    def arrive(h, g):
        groups(x_a.at[h, fives[g]], e_r.at[h * 3 + g]).wait_recv()
        e2_copy(h, fives[g], g).start()

    def take_a(sums, h, g):
        return take(sums, x_a, h, range(5 * g + 1, 5 * g + 6), core)

    def take_b(sums, h, g):
        e2_copy(h, fives[g], g).wait_recv()
        return take(sums, x_b, h, range(5 * g + 1, 5 * g + 6), 1 - core)

    def take_own(h):
        sums = (jnp.zeros((PART, UNITS), F32), jnp.zeros((PART, UNITS), F32), jnp.zeros((PART, 128), F32))
        sums = take(sums, x_a, h, [0], core)
        e2_copy(h, pl.ds(0, 1), 3).wait_recv()
        return take(sums, x_b, h, [0], 1 - core)

    def f_copy(h):
        return remote(act_s.at[core, h], act_s.at[core, h], f_s.at[h], f_r.at[h], sib, z)

    def activate(sums, h):
        gate, up, squares = sums
        square = squares[:, COLS - 128 : COLS - 127] + squares[:, COLS - 127 : COLS - 126]
        factor = lax.rsqrt(square / D + EPSILON)
        g = gate * factor
        u = up * factor
        act_s[core, h] = (g / (1.0 + jnp.exp(-g)) * u).astype(BF16)
        f_copy(h).start()

    def g_copy(m, q):
        return remote(y_out.at[m, q], y_in.at[z * XY + xy], g_s, g_r, core * 16 + m, (z + 1 + q) % 4)

    def g_self(m, q):
        return pltpu.make_async_copy(y_out.at[m, q], y_in.at[z * XY + xy], g_own)

    def results(h, n):
        group = (dp // 4 % 4 + n) % 4
        weight = wcol[PART * h : PART * (h + 1), :1]
        act = jnp.concatenate([act_s[0, h], act_s[1, h]], axis=1)
        for k in range(4):
            m = group * 4 + k
            y = mm(act, down_p[m]) * weight
            low, high = y[:, :128], y[:, 128:]
            for q in range(2):
                at_q = slice(CAP * q, CAP * (q + 1))
                slab = jnp.concatenate([low[at_q], high[at_q]], axis=0)
                y_out[m, 2 * h + q] = slab.astype(BF16)
        for q in ((1, 0) if h == 0 else (2, 3)):
            for i in range(4):
                m = group * 4 + (dp + i) % 4
                if n == 0 and i == 0 and q == 3:
                    to_self = core * 16 + m == dp

                    @pl.when(to_self)
                    def _():
                        g_self(m, q).start()

                    @pl.when(jnp.logical_not(to_self))
                    def _():
                        g_copy(m, q).start()

                else:
                    g_copy(m, q).start()

    sums = take_own(0)
    for g in range(3):
        arrive(0, g)
        sums = take_a(sums, 0, g)
    for g in range(3):
        sums = take_b(sums, 0, g)
    activate(sums, 0)
    sums = take_own(1)
    f_copy(0).wait_recv()
    results(0, 3)
    arrive(1, 0)
    results(0, 2)
    arrive(1, 1)
    results(0, 1)
    arrive(1, 2)
    results(0, 0)
    sums = take_a(sums, 1, 0)
    sums = take_b(sums, 1, 0)
    sums = take_a(sums, 1, 1)
    sums = take_b(sums, 1, 1)
    sums = take_a(sums, 1, 2)
    sums = take_b(sums, 1, 2)
    activate(sums, 1)
    f_copy(1).wait_recv()
    for n in (3, 2, 1, 0):
        results(1, n)
    mine = side == core

    def slabs(count):
        return remote(y_in.at[pl.ds(0, count)], y_in.at[pl.ds(0, count)], g_s, g_r, sib, z)


    left(heads_a.at[pl.ds(0, 15)], a_s)
    left(heads_a, a2_s)
    left(hidden.at[pl.ds(0, 3)], hid_s)
    w_copy.wait_send()
    left(part_in.at[1, pl.ds(0, 3)], c_s.at[1])
    for n in range(2, 6):
        left(x_out.at[1, pl.ds(0, 5)], e_s.at[n])
    left(x_a, e2_s)
    for h in range(2):
        f_copy(h).wait_send()

    @pl.when(mine)
    def _():
        slabs(63).wait_recv()
        g_self(0, 0).wait()

    @pl.when(jnp.logical_not(mine))
    def _():
        slabs(64).wait_recv()

    total = jnp.zeros((2 * QTOK, 128), F32)
    for j in range(4):
        total = total + mm(merge[...], y_in[XY * j : XY * (j + 1)].reshape(XY * 2 * CAP, 128))
    total = jnp.concatenate([total[:QTOK], total[QTOK:, : COLS - 128]], axis=1)
    out[...] = (mid_s[...] + total).astype(BF16)

    @pl.when(mine)
    def _():
        slabs(63).wait_send()

    @pl.when(jnp.logical_not(mine))
    def _():
        slabs(64).wait_send()


def on_device(
    query, new_latent, cache, cache_len, w_uv, w_out, hidden_in, norm_gain, routing, route_weight,
    w_gate_up, w_down,
):
    vmem = pl.BlockSpec(memory_space=pltpu.VMEM)
    hbm = pl.BlockSpec(memory_space=pl.ANY)
    dma = pltpu.SemaphoreType.DMA
    return pl.pallas_call(
        kernel,
        out_shape=jax.ShapeDtypeStruct((QTOK, COLS), BF16),
        in_specs=[hbm] * 12,
        out_specs=vmem,
        scratch_shapes=[
            pltpu.VMEM((4, 16, LAT), BF16),
            pltpu.VMEM((4, LAT), BF16),
            pltpu.SMEM((2,), jnp.int32),
            pltpu.VMEM((QTOK, COLS), BF16),
            pltpu.VMEM((1, COLS), F32),
            pltpu.VMEM((TOP, TOKENS), jnp.int32),
            pltpu.VMEM((TOP, TOKENS), F32),
            pltpu.VMEM((2, LAT, MAXLEN), BF16),
            pltpu.VMEM((16, KVL, VH), BF16),
            pltpu.VMEM((COLS, 16 * VH), BF16),
            pltpu.VMEM((2, D, UNITS), BF16),
            pltpu.VMEM((2, UNITS, HALF), BF16),
            pltpu.VMEM((XY, 2 * UNITS, WIDE), BF16),
            pltpu.VMEM((XY, 64, VH), BF16),
            pltpu.VMEM((XY, 64, VH), BF16),
            pltpu.VMEM((32 * 64, VH), F32),
            pltpu.VMEM((4, QTOK, COLS), F32),
            pltpu.VMEM((5, QTOK, WIDE), BF16),
            pltpu.VMEM((2, 4, 2, QTOK, WIDE), BF16),
            pltpu.VMEM((4, QTOK, WIDE), BF16),
            pltpu.VMEM((2, XY, PART, 2 * QTOK), BF16),
            pltpu.VMEM((EXPERTS, TOKENS), F32),
            pltpu.VMEM((EXPERTS, TOKENS), F32),
            pltpu.VMEM((QTOK, COLS), F32),
            pltpu.VMEM((ROWS, 128), F32),
            pltpu.VMEM((2 * QTOK, XY * 2 * CAP), BF16),
            pltpu.VMEM((2, XY, PART, WIDE), BF16),
            pltpu.VMEM((2, XY, PART, WIDE), BF16),
            pltpu.VMEM((2, XY, PART, WIDE), BF16),
            pltpu.VMEM((2, 2, PART, UNITS), BF16),
            pltpu.VMEM((XY, 4, 2 * CAP, 128), BF16),
            pltpu.VMEM((4 * XY, 2 * CAP, 128), BF16),
            dma((13,)),
            dma, dma, dma, dma,
            dma, dma((3,)), dma, dma((4,)),
            dma((2,)), dma((8,)),
            dma((6,)), dma((6,)), dma, dma((8,)),
            dma((2,)), dma((2,)), dma, dma, dma,
        ],
        compiler_params=pltpu.CompilerParams(
            collective_id=0, has_side_effects=True, vmem_limit_bytes=56 * 2**20
        ),
    )(
        query, new_latent, cache.transpose(0, 2, 1), cache_len, w_uv, w_out.T, hidden_in,
        norm_gain.reshape(1, COLS), routing.T, route_weight.T, w_gate_up, w_down,
    )


def solution(mesh):
    placed = (
        P("dp", "tp", None),
        P("dp", None),
        P("dp", None, None),
        P("dp"),
        P("tp", None, None),
        P("tp", "dp"),
        P("tp", "dp"),
        P("dp"),
        P(),
        P(),
        P(None, None, ("dp", "tp")),
        P(("dp", "tp"), None),
    )
    return jax.shard_map(
        on_device, mesh=mesh, in_specs=placed, out_specs=P("tp", "dp"), check_vma=False
    )
```
